32 devices in a mesh: section: 2 (over x), dp: 16 (over z, y, core).
Axes of the slice: x: 2, y: 2, z: 4, core: 2. Of those that a mesh axis runs over, the one named last changes fastest.
Arguments:
- patches: bfloat16 [2048, 768], P('dp'), may hold values from -6 to 6
- cotangent: bfloat16 [2048, 768], P('dp'), may hold values from -6 to 6
- seg_ids: int32 [2048], P('dp'), may hold values from -1 to 3, as said below
- grid_cols: int32 [32, 4], P('dp'), may hold values from 1 to 8
- norm_gain1: float32 [2, 768], P('section'), may hold values from 0.5 to 1.5
- norm_bias1: float32 [2, 768], P('section'), may hold values from -3 to 3
- qkv_weight: bfloat16 [2, 768, 2304], P('section'), may hold values from -0.21875 to 0.21875
- out_weight: bfloat16 [2, 768, 768], P('section'), may hold values from -1.75 to 1.75
- out_bias: float32 [2, 768], P('section'), may hold values from -2 to 2
- attn_scale: float32 [2, 768], P('section'), may hold values from 0.5 to 1.5
- norm_gain2: float32 [2, 768], P('section'), may hold values from 0.5 to 1.5
- norm_bias2: float32 [2, 768], P('section'), may hold values from -3 to 3
- up_weight: bfloat16 [2, 768, 3072], P('section'), may hold values from -0.21875 to 0.21875
- up_bias: float32 [2, 3072], P('section'), may hold values from -3 to 3
- down_weight: bfloat16 [2, 3072, 768], P('section'), may hold values from -0.109375 to 0.109375
- down_bias: float32 [2, 768], P('section'), may hold values from -2 to 2
- mlp_scale: float32 [2, 768], P('section'), may hold values from 0.5 to 1.5
- rel_table: float32 [2, 2, 12, 31], P('section'), may hold values from -4 to 4
Outputs:
- section_out: float32 [2, 2048, 768], P('section', 'dp')
- section_grad: float32 [2, 2048, 768], P('section', 'dp')
- grad_norm_gain1: float32 [2, 768], P('section', 'dp')
- grad_norm_bias1: float32 [2, 768], P('section', 'dp')
- grad_qkv_weight: float32 [2, 768, 2304], P('section', 'dp')
- grad_out_weight: float32 [2, 768, 768], P('section', 'dp')
- grad_out_bias: float32 [2, 768], P('section', 'dp')
- grad_attn_scale: float32 [2, 768], P('section', 'dp')
- grad_norm_gain2: float32 [2, 768], P('section', 'dp')
- grad_norm_bias2: float32 [2, 768], P('section', 'dp')
- grad_up_weight: float32 [2, 768, 3072], P('section', 'dp')
- grad_up_bias: float32 [2, 3072], P('section', 'dp')
- grad_down_weight: float32 [2, 3072, 768], P('section', 'dp')
- grad_down_bias: float32 [2, 768], P('section', 'dp')
- grad_mlp_scale: float32 [2, 768], P('section', 'dp')
- grad_rel_table: float32 [2, 2, 12, 31], P('section')
The draws below stay inside these ranges and needn't reach their ends.
Inputs may be any that keep to these rules, and one draw needn't show every extreme that they name: `seg_ids`: each sequence of 64 positions holds pages 0 to 3 in this order, page p a whole grid of whole rows of grid_cols[p] patches laid out row by row, then padding marked -1.
All inputs are finite; a program needn't handle non-finite values.
Results may differ from the reference program's by a relative error of at most 0.017.
Values sent between devices are 32-bit elements; how exact they have to be, the bound alone decides.
No kernel may reach another device: no remote copies, remote signals or barrier semaphores. Data moves between devices by JAX's collectives and lax.ppermute only.
A program may use at most 256 MiB of HBM per device.

```python
import math
import jax
import jax.numpy as jnp
from jax import lax

D = 768
HEADS = 12
HEAD = 64
FF = 3072
SEQ = 64
PAGES = 4
CMAX = 8
RMAX = 15
NR = 31
SEQS = 32
TOKENS = 2048
N_SECTION = 2


def page_layout(key):
    width_key, height_key = jax.random.split(key)
    columns = jax.random.randint(width_key, (SEQS, PAGES), 1, CMAX + 1).astype(jnp.int32)
    columns = columns.at[0, 0].set(CMAX).at[0, 1].set(1)
    row_room = (SEQ // PAGES // columns).astype(jnp.int32)
    heights = 1 + jax.random.randint(height_key, (SEQS, PAGES), 0, 1 << 20).astype(jnp.int32) % row_room
    heights = heights.at[0].set(1).astype(jnp.int32)
    page_ends = jnp.cumsum(heights * columns, axis=1).astype(jnp.int32)
    places = jnp.arange(SEQ, dtype=jnp.int32)
    pages_done = jnp.sum((places[None, :, None] >= page_ends[:, None, :]).astype(jnp.int32), axis=2).astype(jnp.int32)
    segment = jnp.where(pages_done >= PAGES, -1, pages_done).astype(jnp.int32)
    return (columns, segment.reshape(SEQS * SEQ))


def draw_seg_ids(key, part):
    return page_layout(key)[1]


def draw_grid_cols(key, part):
    return page_layout(key)[0]


def with_spikes(entries, stream_key, source, target, parts, factor):
    def block_of(dim):
        return (jnp.arange(entries.shape[dim]) // (entries.shape[dim] // parts)).reshape((-1,) + (1,) * (entries.ndim - 1 - dim))

    first = jax.random.permutation(stream_key, parts)[block_of(target)]
    other_side = (block_of(target) + parts // 2) % parts
    return jnp.where((block_of(source) == first) | (block_of(source) == other_side), factor * entries, entries)


def block_scale(own_key, dims, cuts, low, largest):
    level, own = 1.0, jax.random.fold_in(own_key, 6)
    for position, parts in cuts:
        steps = jnp.exp(jax.random.uniform(jax.random.fold_in(own, position), (parts,), jnp.float32, low / len(cuts), largest / len(cuts)))
        level = level * jnp.repeat(steps, dims[position] // parts).reshape([-1 if axis == position else 1 for axis in range(len(dims))])
    return level


def scatter_about(key, shape, scale, bound, pieces=(), kind=jnp.bfloat16):
    gain = block_scale(key, shape, pieces, -0.22, 0.18) if pieces else 1.0
    result = jax.random.normal(key, shape, jnp.float32) * scale * gain
    return jnp.minimum(jnp.maximum(result, -bound), bound).astype(kind)


def bell_draw_with(own_key, extent, spread, reach, cuts, heavy, kind=jnp.bfloat16):
    values = spread * jax.random.normal(own_key, extent, jnp.float32)
    if cuts:
        values = values * block_scale(own_key, extent, cuts, -0.22, 0.18)
    return jnp.clip(with_spikes(values, jax.random.fold_in(own_key, 3), *heavy), -reach, reach).astype(kind)


def setup_inputs(seed: int = 0) -> dict:
    seeds = jax.random.split(jax.random.key(seed), 19)
    patches = scatter_about(seeds[0], (TOKENS, D), 1.0, 6.0, ((0, 16),))
    cotangent = bell_draw_with(seeds[1], (TOKENS, D), 1.0, 6.0, ((0, 16),), (0, 1, 16, 2.0))
    seg_ids = draw_seg_ids(jax.random.fold_in(seeds[18], 71), 0)
    grid_cols = draw_grid_cols(jax.random.fold_in(seeds[18], 71), 0)
    norm_gain1 = jnp.clip(1.0 + 0.1 * jax.random.normal(seeds[4], (N_SECTION, D), jnp.float32), 0.5, 1.5)
    norm_bias1 = scatter_about(seeds[5], (N_SECTION, D), 0.5, 3.0, ((0, 2),), jnp.float32)
    qkv_weight = scatter_about(seeds[6], (N_SECTION, D, 3 * D), D ** -0.5, 0.21875, ((0, 2),))
    out_weight = scatter_about(seeds[7], (N_SECTION, D, D), (D // 64) ** -0.5, 1.75, ((0, 2),))
    out_bias = scatter_about(seeds[8], (N_SECTION, D), 0.3, 2.0, ((0, 2),), jnp.float32)
    attn_scale = jnp.clip(jnp.exp(math.log(1.5) - 1.0986123 * jax.random.uniform(seeds[9], (N_SECTION, D), jnp.float32) ** block_scale(seeds[9], (N_SECTION, D), ((0, 2),), -0.2, 0.2)), 0.5, 1.5)
    norm_gain2 = jnp.clip(1.0 + 0.1 * jax.random.normal(seeds[10], (N_SECTION, D), jnp.float32), 0.5, 1.5)
    norm_bias2 = scatter_about(seeds[11], (N_SECTION, D), 0.5, 3.0, ((0, 2),), jnp.float32)
    up_weight = scatter_about(seeds[12], (N_SECTION, D, FF), D ** -0.5, 0.21875, ((0, 2),))
    up_bias = scatter_about(seeds[13], (N_SECTION, FF), 0.5, 3.0, ((0, 2),), jnp.float32)
    down_weight = scatter_about(seeds[14], (N_SECTION, FF, D), FF ** -0.5, 0.109375, ((0, 2),))
    down_bias = scatter_about(seeds[15], (N_SECTION, D), 0.3, 2.0, ((0, 2),), jnp.float32)
    mlp_scale = jnp.clip(jnp.exp(math.log(1.5) - 1.0986123 * jax.random.uniform(seeds[16], (N_SECTION, D), jnp.float32) ** block_scale(seeds[16], (N_SECTION, D), ((0, 2),), -0.2, 0.2)), 0.5, 1.5)
    rel_table = scatter_about(seeds[17], (N_SECTION, 2, HEADS, NR), 1.0, 4.0, ((0, 2),), jnp.float32)
    return {"patches": patches, "cotangent": cotangent, "seg_ids": seg_ids, "grid_cols": grid_cols, "norm_gain1": norm_gain1, "norm_bias1": norm_bias1, "qkv_weight": qkv_weight, "out_weight": out_weight, "out_bias": out_bias, "attn_scale": attn_scale, "norm_gain2": norm_gain2, "norm_bias2": norm_bias2, "up_weight": up_weight, "up_bias": up_bias, "down_weight": down_weight, "down_bias": down_bias, "mlp_scale": mlp_scale, "rel_table": rel_table}


EPSILON = 1e-06
MASKED = -1e+30

@jax.custom_vjp
def low(v):
    return lax.optimization_barrier(v.astype(jnp.bfloat16)).astype(jnp.float32)

@jax.custom_vjp
def low_back(v):
    return v

def low_keep(v):
    return (low(v), None)

def low_pass(kept, grad):
    return (grad,)

def back_keep(v):
    return (v, None)

def back_low(kept, grad):
    return (low(grad),)
low.defvjp(low_keep, low_pass)
low_back.defvjp(back_keep, back_low)

def layer_normalize(residual_stream):
    average = lax.optimization_barrier(jnp.mean(residual_stream, axis=-1, keepdims=True))
    shifted = residual_stream - average
    return shifted * lax.rsqrt(lax.optimization_barrier(jnp.mean(shifted * shifted, axis=-1, keepdims=True)) + EPSILON)

def grid_places(segment, columns):
    page_count = columns.shape[0]
    seq_length = segment.shape[0]
    member = (segment[:, None] == jnp.arange(page_count, dtype=jnp.int32)[None, :]).astype(jnp.int32)
    counts = lax.optimization_barrier(jnp.sum(member, axis=0)).astype(jnp.int32)
    starts = (jnp.cumsum(counts) - counts).astype(jnp.int32)
    page_start = lax.optimization_barrier(jnp.sum(member * starts[None, :], axis=1)).astype(jnp.int32)
    row_width = jnp.maximum(lax.optimization_barrier(jnp.sum(member * columns[None, :], axis=1)), 1).astype(jnp.int32)
    offset = jnp.arange(seq_length, dtype=jnp.int32) - page_start
    return (offset // row_width, offset % row_width)

def relative_index(segment, columns):
    grid_rows, grid_cols_of = grid_places(segment, columns)
    row_step = (jnp.clip(grid_rows[:, None] - grid_rows[None, :], -RMAX, RMAX) + RMAX).astype(jnp.int32)
    col_step = (jnp.clip(grid_cols_of[:, None] - grid_cols_of[None, :], -RMAX, RMAX) + RMAX).astype(jnp.int32)
    places = jnp.arange(segment.shape[0], dtype=jnp.int32)
    same_page = (segment[:, None] == segment[None, :]) & (segment[None, :] >= 0)
    allowed = same_page | (places[:, None] == places[None, :])
    return (row_step, col_step, allowed)

def attend(packed, table):
    qkv_rows, segment, columns = packed
    row_step, col_step, allowed = relative_index(segment, columns)
    seq_length = qkv_rows.shape[0]
    query_rows = qkv_rows[:, :D].reshape(seq_length, HEADS, HEAD)
    key_rows = qkv_rows[:, D:2 * D].reshape(seq_length, HEADS, HEAD)
    value_rows = qkv_rows[:, 2 * D:].reshape(seq_length, HEADS, HEAD)
    rel_bias = table[0][:, row_step] + table[1][:, col_step]
    score_scale = 1.0 / math.sqrt(HEAD)
    scores = jnp.einsum('ihd,jhd->hij', query_rows, key_rows, precision=lax.Precision.HIGHEST) * score_scale + rel_bias
    scores = low_back(scores)
    scores = jnp.where(allowed[None], scores, MASKED)
    row_top = lax.optimization_barrier(jnp.max(scores, axis=-1, keepdims=True))
    exp_scores = jnp.exp(scores - row_top)
    attn_probs = low(exp_scores / lax.optimization_barrier(jnp.sum(exp_scores, axis=-1, keepdims=True)))
    attn_mixed = jnp.einsum('hij,jhd->ihd', attn_probs, value_rows, precision=lax.Precision.HIGHEST)
    return attn_mixed.reshape(seq_length, D)

def matmul(left, right):
    return jnp.dot(left, right, precision=lax.Precision.HIGHEST, preferred_element_type=jnp.float32)

def layer(residual_stream, params, segments, columns):
    gain_one, bias_one, qkv_weight, out_weight, out_bias, attn_scale, gain_two, bias_two, up_weight, up_bias, down_weight, down_bias, mlp_scale, rel_table = params
    normed = low(layer_normalize(residual_stream) * gain_one + bias_one)
    qkv_all = low_back(low(matmul(normed, qkv_weight)))

    def attend_one(packed):
        return attend(packed, rel_table)
    attn_mixed = lax.map(jax.checkpoint(attend_one), (qkv_all.reshape(-1, SEQ, 3 * D), segments.reshape(-1, SEQ), columns))
    attn_mixed = low_back(low(attn_mixed.reshape(-1, D)))
    branch = low_back(matmul(attn_mixed, out_weight) + out_bias)
    middle_activation = residual_stream + attn_scale * branch
    normed_two = low(layer_normalize(middle_activation) * gain_two + bias_two)
    hidden = low_back(matmul(normed_two, up_weight) + up_bias)
    active = low(jax.nn.gelu(hidden, approximate=True))
    output = low_back(matmul(active, down_weight) + down_bias)
    return middle_activation + mlp_scale * output

def reference(patches, cotangent, seg_ids, grid_cols, norm_gain1, norm_bias1, qkv_weight, out_weight, out_bias, attn_scale, norm_gain2, norm_bias2, up_weight, up_bias, down_weight, down_bias, mlp_scale, rel_table):
    weights = (norm_gain1, norm_bias1, qkv_weight, out_weight, out_bias, attn_scale, norm_gain2, norm_bias2, up_weight, up_bias, down_weight, down_bias, mlp_scale, rel_table)

    def section_params(index):
        return tuple((weight_all[index].astype(jnp.float32) for weight_all in weights))

    def run_layer(residual_stream, params):
        return layer(residual_stream, params, seg_ids, grid_cols)
    layer_zero, pull_zero = jax.vjp(run_layer, patches.astype(jnp.float32), section_params(0))
    layer_one, pull_one = jax.vjp(run_layer, layer_zero, section_params(1))
    grad_middle, grads_one = pull_one(cotangent.astype(jnp.float32))
    grad_first, grads_zero = pull_zero(grad_middle)

    def paired(index):
        return jnp.stack([grads_zero[index], grads_one[index]])
    return (jnp.stack([layer_zero, layer_one]), jnp.stack([grad_first, grad_middle]), paired(0), paired(1), paired(2), paired(3), paired(4), paired(5), paired(6), paired(7), paired(8), paired(9), paired(10), paired(11), paired(12), paired(13))
```

```python
import functools
import math

import jax
import jax.numpy as jnp
from jax import lax
from jax.experimental import pallas as pl
from jax.experimental.pallas import tpu as pltpu
from jax.sharding import PartitionSpec as P

D = 768
HEADS = 12
HEAD = 64
FF = 3072
RMAX = 15
SEQ = 64
ROWS = 128
BLOCK = 8
GROUP = 4 * HEAD
GROUPS = D // GROUP
TILE = 512
TILES = FF // TILE
SEL = D // BLOCK
SELF = FF // BLOCK

EPSILON = 1e-06
MASKED = -1e30
C0 = math.sqrt(2.0 / math.pi)
C1 = C0 * 0.044715
F32 = jnp.float32
BF16 = jnp.bfloat16


def dot(left, right):
    return lax.dot_general(left, right, (((1,), (0,)), ((), ())), preferred_element_type=F32)


def dot_rt(left, right):
    return lax.dot_general(left, right, (((1,), (1,)), ((), ())), preferred_element_type=F32)


def dot_lt(left, right):
    return lax.dot_general(left, right, (((0,), (0,)), ((), ())), preferred_element_type=F32)


def normalize(rows):
    shifted = rows - jnp.mean(rows, axis=-1, keepdims=True)
    inverse = lax.rsqrt(jnp.mean(shifted * shifted, axis=-1, keepdims=True) + EPSILON)
    return shifted * inverse, inverse


def normalize_back(grad, normal, inverse):
    mean_grad = jnp.mean(grad, axis=-1, keepdims=True)
    mean_both = jnp.mean(grad * normal, axis=-1, keepdims=True)
    return (grad - mean_grad - normal * mean_both) * inverse


def column_sum(rows):
    return jnp.sum(rows, axis=0, keepdims=True)


def prepare_kernel(info, seg, cols, patches, cotangent, out):
    section = info[0]
    out[:ROWS, :] = jnp.where(section == 0, patches[...].astype(F32), cotangent[...].astype(F32))
    segment = seg[...]
    lane = lax.broadcasted_iota(jnp.int32, (1, ROWS), 1)
    place = (lane % SEQ).astype(F32)
    second = lane >= SEQ
    start = jnp.zeros((1, ROWS), F32)
    width = jnp.zeros((1, ROWS), F32)
    before_first = jnp.zeros((1, 1), F32)
    before_second = jnp.zeros((1, 1), F32)
    for page in range(cols.shape[1]):
        member = segment == page
        ones = member.astype(F32)
        start += jnp.where(member, jnp.where(second, before_second, before_first), 0.0)
        width += jnp.where(member, jnp.where(second, cols[1, page], cols[0, page]).astype(F32), 0.0)
        before_first += jnp.sum(jnp.where(second, 0.0, ones), axis=1, keepdims=True)
        before_second += jnp.sum(jnp.where(second, ones, 0.0), axis=1, keepdims=True)
    width = jnp.maximum(width, 1.0)
    offset = place - start
    grid_row = jnp.floor((offset + 0.5) / width)
    grid_col = offset - grid_row * width
    line = lax.broadcasted_iota(jnp.int32, (8, ROWS), 0)
    out[ROWS:, :] = jnp.zeros((8, D), F32)
    out[ROWS:, :ROWS] = jnp.where(
        line == 0, segment.astype(F32), jnp.where(line == 1, grid_row, grid_col)
    )


def steps_of(meta, part):
    shape = (SEQ, ROWS)
    lane = lax.broadcasted_iota(jnp.int32, shape, 1)
    line = lax.broadcasted_iota(jnp.int32, shape, 0)
    left = lane < SEQ

    def across(values):
        wide = jnp.broadcast_to(values, (8, ROWS))
        swapped = pltpu.roll(wide, SEQ, 1)
        low = lax.broadcasted_iota(jnp.int32, (8, ROWS), 1) < SEQ
        both = jnp.where(low, wide, swapped) if part == 0 else jnp.where(low, swapped, wide)
        return both[:1]

    def down(values):
        return jnp.broadcast_to(values, (ROWS, ROWS)).T[part * SEQ : (part + 1) * SEQ, :]

    seg_i, row_i, col_i = (across(meta[k : k + 1]) for k in range(3))
    seg_j, row_j, col_j = (down(meta[k : k + 1]) for k in range(3))
    allowed = ((seg_i == seg_j) & (seg_j >= 0.0)) | ((lane % SEQ) == line)
    base = jnp.where(left, RMAX, RMAX + SEQ)
    row_step = jnp.clip(row_i - row_j, -RMAX, RMAX).astype(jnp.int32) + base
    col_step = jnp.clip(col_i - col_j, -RMAX, RMAX).astype(jnp.int32) + base
    return row_step, col_step, allowed


def fill_bias(meta, tabs, bias, first):
    for part in range(2):
        row_step, col_step, allowed = steps_of(meta, part)
        for pair in range(HEADS // 2):
            by_row = jnp.broadcast_to(tabs[pair : pair + 1, :], (SEQ, ROWS))
            by_col = jnp.broadcast_to(tabs[6 + pair : 7 + pair, :], (SEQ, ROWS))
            both = jnp.take_along_axis(by_row, row_step, axis=1) + jnp.take_along_axis(
                by_col, col_step, axis=1
            )
            bias[first + part, :, pair * ROWS : (pair + 1) * ROWS] = jnp.where(allowed, both, MASKED)


def diagonal_mask():
    line = lax.broadcasted_iota(jnp.int32, (GROUP, GROUP), 0) // HEAD
    lane = lax.broadcasted_iota(jnp.int32, (GROUP, GROUP), 1) // HEAD
    return line == lane


def spread(block, mask):
    return jnp.where(mask, jnp.concatenate([block] * 4, axis=0), jnp.zeros((), block.dtype))


def gather_diagonal(full):
    lane = lax.broadcasted_iota(jnp.int32, (SEQ, GROUP), 1) // HEAD
    result = full[:SEQ]
    for head in range(1, 4):
        result = jnp.where(lane == head, full[head * SEQ : (head + 1) * SEQ], result)
    return result


def layer_kernel(kind, shards, first_call, *refs):
    refs = list(refs)

    def take(count):
        taken = refs[:count]
        del refs[:count]
        return taken

    rows = shards * ROWS
    seqs = 2 * shards
    (info,) = take(1)
    gain1, bias1, out_bias, attn_scale, gain2, bias2, up_bias, down_bias, mlp_scale, tabs = take(10)
    weights = take(4)
    a_refs = take(shards)
    b_refs = take(shards) if kind != "fwd" else []
    sums_in = take(5) if kind == "chunk" and not first_call else []
    if kind == "fwd":
        (y_out,) = take(1)
    elif kind == "own":
        y_out, grad_out, part_out, ds_out = take(4)
    else:
        sums_out = take(5)
    wq, wo, wu, wd, sems = take(5)
    qkv, bias, probs, mixed, middle, branch, n2b = take(7)
    if kind != "fwd":
        dob, dn2, dmix, dqkv, normed = take(5)
    if kind != "chunk":
        (total,) = take(1)
    else:
        active, sums, sum_sems = take(3)
    section = info[0]
    place = info[1]

    def first_copy(k):
        if k == 3:
            return pltpu.make_async_copy(weights[1], wo, sems.at[3])
        span = pl.ds(k * D, D)
        return pltpu.make_async_copy(weights[0].at[:, span], wq.at[:, span], sems.at[k])

    def up_copy(k):
        span = pl.ds(pl.multiple_of(k * TILE, TILE), TILE)
        return pltpu.make_async_copy(weights[2].at[:, span], wu.at[:, span], sems.at[4 + k])

    def down_copy(k):
        span = pl.ds(pl.multiple_of(k * TILE, TILE), TILE)
        return pltpu.make_async_copy(weights[3].at[span, :], wd.at[span, :], sems.at[4 + TILES + k])

    def run():
        for k in range(4):
            first_copy(k).start()
        for k in range(TILES):
            up_copy(k).start()
            down_copy(k).start()
        if sums_in:
            for k in range(5):
                pltpu.make_async_copy(sums_in[k], sums[k], sum_sems.at[k]).start()

        def layer_input(k):
            if kind == "fwd":
                return a_refs[k][:ROWS, :]
            return jnp.where(section == 0, a_refs[k][:ROWS, :], b_refs[k][...])

        def upstream(k):
            return jnp.where(section == 0, b_refs[k][...], a_refs[k][:ROWS, :])

        def whole(pick):
            pieces = [pick(k) for k in range(shards)]
            return pieces[0] if shards == 1 else jnp.concatenate(pieces, axis=0)

        normal, _ = normalize(whole(layer_input))
        normed_value = (normal * gain1[...] + bias1[...]).astype(BF16)
        if kind != "fwd":
            normed[...] = normed_value
            dob[...] = (mlp_scale[...] * whole(upstream)).astype(BF16)
        for k in range(3):
            first_copy(k).wait()
            qkv[:, k * D : (k + 1) * D] = dot(normed_value, wq[:, k * D : (k + 1) * D]).astype(BF16)
        for k in range(shards):
            fill_bias(a_refs[k][ROWS:, :ROWS], tabs, bias, 2 * k)
        mask = diagonal_mask()

        def attend(s, carry):
            span = pl.ds(pl.multiple_of(s * SEQ, SEQ), SEQ)
            for g in range(GROUPS):
                cols = slice(g * GROUP, (g + 1) * GROUP)
                query = qkv[span, g * GROUP : (g + 1) * GROUP] * BF16(0.125)
                key = qkv[span, D + g * GROUP : D + (g + 1) * GROUP]
                value = qkv[span, 2 * D + g * GROUP : 2 * D + (g + 1) * GROUP]
                scores = dot_rt(key, spread(query, mask)) + bias[s, :, cols]
                grown = jnp.exp(scores - jnp.max(scores, axis=0, keepdims=True))
                prob = grown / jnp.sum(grown, axis=0, keepdims=True)
                if kind != "fwd":
                    probs[s, :, cols] = prob
                mixed[span, cols] = gather_diagonal(dot_lt(prob.astype(BF16), value)).astype(BF16)
            return carry

        lax.fori_loop(0, seqs, attend, 0)
        first_copy(3).wait()
        branch_value = dot(mixed[...], wo[...]) + out_bias[...]
        branch[...] = branch_value
        middle_value = whole(layer_input) + attn_scale[...] * branch_value
        middle[...] = middle_value
        normal2, _ = normalize(middle_value)
        n2b[...] = (normal2 * gain2[...] + bias2[...]).astype(BF16)
        if kind == "chunk":
            line = lax.broadcasted_iota(jnp.int32, (SEL, D), 0)
            lane = lax.broadcasted_iota(jnp.int32, (SEL, D), 1)
            pick = (lane == line + place * SEL).astype(BF16)
            normed_sel = dot_rt(pick, normed[...]).astype(BF16)
            mixed_sel = dot_rt(pick, mixed[...]).astype(BF16)
            n2_sel = dot_rt(pick, n2b[...]).astype(BF16)
            sum_q, sum_o, sum_u, sum_d, sum_v = sums
            if sums_in:
                for k in range(5):
                    pltpu.make_async_copy(sums_in[k], sums[k], sum_sems.at[k]).wait()
            else:
                for ref in sums:
                    ref[...] = jnp.zeros(ref.shape, F32)
        if kind != "chunk":
            total[...] = jnp.zeros((rows, D), F32)
        if kind != "fwd":
            dn2[...] = jnp.zeros((rows, D), F32)

        def feed(k, carry):
            up_copy(k).wait()
            down_copy(k).wait()
            span = pl.ds(pl.multiple_of(k * TILE, TILE), TILE)
            hidden = dot(n2b[...], wu[:, span]) + up_bias[:, span]
            square = hidden * hidden
            bend = jnp.tanh(hidden * (C0 + C1 * square))
            half = 0.5 + 0.5 * bend
            act = (hidden * half).astype(BF16)
            if kind != "chunk":
                total[...] += dot(act, wd[span, :])
            else:
                active[:, span] = act
            if kind != "fwd":
                d_act = dot_rt(dob[...], wd[span, :])
                slope = half + hidden * (0.5 - 0.5 * bend * bend) * (C0 + 3.0 * C1 * square)
                d_hid = (slope * d_act).astype(BF16)
                dn2[...] += dot_rt(d_hid, wu[:, span])
                if kind == "chunk":
                    sum_u[:, span] += dot(n2_sel, d_hid)
                    sum_v[pl.ds(8 + k, 1), :TILE] += column_sum(d_hid.astype(F32))
            return carry

        lax.fori_loop(0, TILES, feed, 0)
        if kind != "chunk":
            output = total[...] + down_bias[...]
            y_out[...] = middle[...] + mlp_scale[...] * output
        if kind == "fwd":
            return
        up = whole(upstream)
        normal2, inverse2 = normalize(middle[...])
        d_n2 = dn2[...]
        d_middle = up + normalize_back(d_n2 * gain2[...], normal2, inverse2)
        d_branch = (attn_scale[...] * d_middle).astype(BF16)
        if kind == "own":
            part_out[0:1, :] = column_sum(up * output)
            grad_out[...] = d_middle
        else:
            sum_v[0:1, :] += column_sum(dob[...].astype(F32))
            sum_v[1:2, :] += column_sum(d_n2 * normal2)
            sum_v[2:3, :] += column_sum(d_n2)
            sum_v[3:4, :] += column_sum(d_middle * branch[...])
            sum_v[4:5, :] += column_sum(d_branch.astype(F32))
            sum_o[...] += dot(mixed_sel, d_branch)
            chosen = active[:, pl.ds(pl.multiple_of(place * SELF, ROWS), SELF)]
            sum_d[...] += dot_lt(chosen, dob[...])
        dmix[...] = dot_rt(d_branch, wo[...]).astype(BF16)

        def attend_back(s, carry):
            span = pl.ds(pl.multiple_of(s * SEQ, SEQ), SEQ)
            for g in range(GROUPS):
                cols = slice(g * GROUP, (g + 1) * GROUP)
                query = spread(qkv[span, g * GROUP : (g + 1) * GROUP] * BF16(0.125), mask)
                key = qkv[span, D + g * GROUP : D + (g + 1) * GROUP]
                value = qkv[span, 2 * D + g * GROUP : 2 * D + (g + 1) * GROUP]
                d_mix = spread(dmix[span, cols], mask)
                prob = probs[s, :, cols]
                d_prob = dot_rt(value, d_mix)
                delta = jnp.sum(prob * d_prob, axis=0, keepdims=True)
                d_score = (prob * (d_prob - delta)).astype(BF16)
                d_key = dot(d_score, query)
                d_value = dot(prob.astype(BF16), d_mix)
                d_query = gather_diagonal(dot_lt(d_score, key)) * 0.125
                dqkv[span, g * GROUP : (g + 1) * GROUP] = d_query.astype(BF16)
                dqkv[span, D + g * GROUP : D + (g + 1) * GROUP] = d_key.astype(BF16)
                dqkv[span, 2 * D + g * GROUP : 2 * D + (g + 1) * GROUP] = d_value.astype(BF16)
                if kind == "own":
                    ds_out[s, :, cols] = d_score
            return carry

        lax.fori_loop(0, seqs, attend_back, 0)
        if kind == "own":
            d_normed = dot_rt(dqkv[...], wq[...])
            normal, inverse = normalize(whole(layer_input))
            part_out[1:2, :] = column_sum(d_normed * normal)
            part_out[2:3, :] = column_sum(d_normed)
            grad_out[...] += normalize_back(d_normed * gain1[...], normal, inverse)
        else:
            sum_q[...] += dot(normed_sel, dqkv[...])
            for k in range(5):
                pltpu.make_async_copy(sums[k], sums_out[k], sum_sems.at[k]).start()
            for k in range(5):
                pltpu.make_async_copy(sums[k], sums_out[k], sum_sems.at[k]).wait()

    if kind == "fwd":
        pl.when(section == 0)(run)
    elif kind == "own":
        pl.when(section == first_call)(run)
    else:
        run()


def run_layer(kind, info, params, weights, a_shards, b_shards, sums=None, turn=0):
    shards = len(a_shards)
    rows = shards * ROWS
    seqs = 2 * shards
    vmem = pl.BlockSpec(memory_space=pltpu.VMEM)
    smem = pl.BlockSpec(memory_space=pltpu.SMEM)
    hbm = pl.BlockSpec(memory_space=pl.ANY)
    ins = [info, *params, *weights, *a_shards, *b_shards]
    in_specs = [smem] + [vmem] * len(params) + [hbm] * 4 + [vmem] * (shards + len(b_shards))
    scratch = [
        pltpu.VMEM((D, 3 * D), BF16),
        pltpu.VMEM((D, D), BF16),
        pltpu.VMEM((D, FF), BF16),
        pltpu.VMEM((FF, D), BF16),
        pltpu.SemaphoreType.DMA((4 + 2 * TILES,)),
        pltpu.VMEM((rows, 3 * D), BF16),
        pltpu.VMEM((seqs, SEQ, D), F32),
        pltpu.VMEM((seqs, SEQ, D), F32),
        pltpu.VMEM((rows, D), BF16),
        pltpu.VMEM((rows, D), F32),
        pltpu.VMEM((rows, D), F32),
        pltpu.VMEM((rows, D), BF16),
    ]
    if kind != "fwd":
        scratch += [
            pltpu.VMEM((rows, D), BF16),
            pltpu.VMEM((rows, D), F32),
            pltpu.VMEM((rows, D), BF16),
            pltpu.VMEM((rows, 3 * D), BF16),
            pltpu.VMEM((rows, D), BF16),
        ]
    aliases = {}
    row_shape = jax.ShapeDtypeStruct((ROWS, D), F32)
    if kind == "fwd":
        outs, out_specs, first = (row_shape,), (vmem,), True
    elif kind == "own":
        outs = (
            row_shape,
            row_shape,
            jax.ShapeDtypeStruct((8, D), F32),
            jax.ShapeDtypeStruct((2, SEQ, D), BF16),
        )
        out_specs, first = (vmem,) * 4, turn
    else:
        shapes = [(SEL, 3 * D), (SEL, D), (SEL, FF), (SELF, D), (16, D)]
        outs = tuple(jax.ShapeDtypeStruct(shape, F32) for shape in shapes)
        out_specs = (hbm,) * 5
        first = sums is None
        if not first:
            aliases = {len(ins) + k: k for k in range(5)}
            ins += list(sums)
            in_specs += [hbm] * 5
    if kind != "chunk":
        scratch += [pltpu.VMEM((rows, D), F32)]
    else:
        scratch += [
            pltpu.VMEM((rows, FF), BF16),
            [pltpu.VMEM(shape, F32) for shape in shapes],
            pltpu.SemaphoreType.DMA((5,)),
        ]
    flops = 2 * rows * (3 * D * D + D * D + 2 * D * FF) * (1 if kind == "fwd" else 2)
    return pl.pallas_call(
        functools.partial(layer_kernel, kind, shards, first),
        out_shape=outs,
        in_specs=in_specs,
        out_specs=out_specs,
        scratch_shapes=scratch,
        input_output_aliases=aliases,
        compiler_params=pltpu.CompilerParams(vmem_limit_bytes=52 * 1024 * 1024),
        cost_estimate=pl.CostEstimate(
            flops=flops, bytes_accessed=15_000_000, transcendentals=rows * FF
        ),
        name="layer_" + kind,
    )(*ins)


def table_kernel(info, own, ds1, ds2, part1, part2, out, rows_of):
    section = info[0]
    out[...] = jnp.zeros(out.shape, F32)
    out[0:8, :] = jnp.where(section == 0, part2[...], part1[...])
    rows_of[...] = jnp.zeros(rows_of.shape, F32)
    meta = own[ROWS:, :ROWS]
    lane = lax.broadcasted_iota(jnp.int32, (SEQ, ROWS), 1)
    for part in range(2):
        row_step, col_step, _ = steps_of(meta, part)
        row_step -= jnp.where(lane < SEQ, 0, SEQ)
        col_step -= jnp.where(lane < SEQ, 0, SEQ)
        for pair in range(HEADS // 2):
            span = slice(pair * ROWS, (pair + 1) * ROWS)
            grads = jnp.where(section == 0, ds2[part, :, span], ds1[part, :, span]).astype(F32)
            for r in range(2 * RMAX + 1):
                rows_of[r : r + 1, span] += column_sum(jnp.where(row_step == r, grads, 0.0))
                rows_of[32 + r : 33 + r, span] += column_sum(jnp.where(col_step == r, grads, 0.0))
    line = lax.broadcasted_iota(jnp.int32, (16, D), 0)
    head = lax.broadcasted_iota(jnp.int32, (16, D), 1) // HEAD
    ones = (line == head).astype(F32)
    out[8:24, : 2 * 32] = lax.dot_general(
        ones,
        rows_of[...],
        (((1,), (1,)), ((), ())),
        precision=lax.Precision.HIGHEST,
        preferred_element_type=F32,
    )


def body(
    patches,
    cotangent,
    seg_ids,
    grid_cols,
    norm_gain1,
    norm_bias1,
    qkv_weight,
    out_weight,
    out_bias,
    attn_scale,
    norm_gain2,
    norm_bias2,
    up_weight,
    up_bias,
    down_weight,
    down_bias,
    mlp_scale,
    rel_table,
):
    dp_count = lax.axis_size("dp")
    supers = dp_count // (2 * BLOCK)
    section = lax.axis_index("section")
    device = lax.axis_index("dp")
    core = device % 2
    place = device // (2 * supers)
    info = jnp.stack([section, place]).astype(jnp.int32)
    vmem = pl.BlockSpec(memory_space=pltpu.VMEM)
    smem = pl.BlockSpec(memory_space=pltpu.SMEM)

    def pairs(move):
        return [
            (2 * (b * supers + s) + c, 2 * (move(b) * supers + s) + c)
            for b in range(BLOCK)
            for s in range(supers)
            for c in range(2)
        ]

    def along(array, step):
        return lax.ppermute(array, "dp", pairs(lambda b: (b // 2 + step) % 4 * 2 + b % 2))

    def across(array):
        return lax.ppermute(array, "dp", pairs(lambda b: b ^ 1))

    def sibling(array):
        return lax.ppermute(array, "dp", [(d, d ^ 1) for d in range(dp_count)])

    own = pl.pallas_call(
        prepare_kernel,
        out_shape=jax.ShapeDtypeStruct((ROWS + 8, D), F32),
        in_specs=[smem, vmem, smem, vmem, vmem],
        out_specs=vmem,
        name="prepare",
    )(info, seg_ids.reshape(1, ROWS), grid_cols, patches, cotangent)
    tabs = jnp.pad(rel_table[0], ((0, 0), (0, 0), (0, SEQ - rel_table.shape[3]))).reshape(
        HEADS, 2 * SEQ
    )
    params = (
        norm_gain1,
        norm_bias1,
        out_bias,
        attn_scale,
        norm_gain2,
        norm_bias2,
        up_bias,
        down_bias,
        mlp_scale,
        tabs,
    )
    weights = (qkv_weight[0], out_weight[0], up_weight[0], down_weight[0])

    def gather_all(shard):
        across_own = across(shard)
        moved = [along(shard, step) for step in (1, 3, 2)]
        return [shard, across_own] + moved + [across(piece) for piece in moved]

    a_all = gather_all(own)
    (y0,) = run_layer("fwd", info, params, weights, [own], [])
    x1 = lax.ppermute(y0, "section", [(0, 1)])
    y1, grad1, part1, ds1 = run_layer("own", info, params, weights, [own], [x1], turn=1)
    u0 = lax.ppermute(grad1, "section", [(1, 0)])
    b_own = jnp.where(section == 0, u0, x1)
    b_all = gather_all(b_own)
    _, grad0, part0, ds0 = run_layer("own", info, params, weights, [own], [b_own], turn=0)
    sums = None
    for k in range(0, BLOCK, 2):
        sums = run_layer("chunk", info, params, weights, a_all[k : k + 2], b_all[k : k + 2], sums)

    small = pl.pallas_call(
        table_kernel,
        out_shape=jax.ShapeDtypeStruct((24, D), F32),
        in_specs=[smem] + [vmem] * 5,
        out_specs=vmem,
        scratch_shapes=[pltpu.VMEM((64, D), F32)],
        name="table",
    )(info, own, ds1, ds0, part1, part0)
    small = small + along(small, 1) + along(small, 2) + along(small, 3)
    small = small + across(small)
    sum_q, sum_o, sum_u, sum_d, sum_v = sums
    vectors = jnp.concatenate([sum_v, small], axis=0)
    vectors = vectors + sibling(vectors)
    per_sup = supers

    def across_supers(parts):
        mine = device // 2 % supers
        total = lax.dynamic_index_in_dim(parts, mine, 0, keepdims=False)
        for step in range(1, per_sup):
            sent = lax.dynamic_index_in_dim(parts, (mine + step) % supers, 0, keepdims=False)
            moves = [
                (2 * (b * supers + s) + c, 2 * (b * supers + (s + step) % supers) + c)
                for b in range(BLOCK)
                for s in range(supers)
                for c in range(2)
            ]
            total = total + lax.ppermute(sent, "dp", moves)
        return total

    def scatter(partial):
        parts = partial.reshape(supers, 2, partial.shape[0] // (2 * supers), partial.shape[1])
        kept = lax.dynamic_index_in_dim(parts, core, 1, keepdims=False)
        sent = lax.dynamic_index_in_dim(parts, 1 - core, 1, keepdims=False)
        return across_supers(kept + sibling(sent))[None]

    if supers > 1:
        moves = lambda step: [
            (2 * (b * supers + s) + c, 2 * (b * supers + (s + step) % supers) + c)
            for b in range(BLOCK)
            for s in range(supers)
            for c in range(2)
        ]
        vectors = vectors + sum(
            lax.ppermute(vectors, "dp", moves(step)) for step in range(1, supers)
        )
    width = D // dp_count

    def vector(row):
        return lax.dynamic_slice(vectors, (row, device * width), (1, width))

    grad_up_bias = lax.dynamic_slice(
        vectors[8 : 8 + TILES, :TILE].reshape(1, FF), (0, device * (FF // dp_count)), (1, FF // dp_count)
    )
    table = vectors[24 : 24 + HEADS, :64].reshape(HEADS, 2, 32)[:, :, : 2 * RMAX + 1]
    grad_table = table.transpose(1, 0, 2)[None]
    section_out = jnp.where(section == 0, y0, y1)[None]
    section_grad = jnp.where(section == 0, grad0, grad1)[None]
    return (
        section_out,
        section_grad,
        vector(17),
        vector(18),
        scatter(sum_q),
        scatter(sum_o),
        vector(4),
        vector(3),
        vector(1),
        vector(2),
        scatter(sum_u),
        grad_up_bias,
        scatter(sum_d),
        vector(0),
        vector(16),
        grad_table,
    )


def solution(mesh):
    row, whole = P("dp", None), P("section", None)
    matrix = P("section", None, None)
    in_specs = (
        row,
        row,
        P("dp"),
        row,
        whole,
        whole,
        matrix,
        matrix,
        whole,
        whole,
        whole,
        whole,
        matrix,
        whole,
        matrix,
        whole,
        whole,
        P("section", None, None, None),
    )
    tokens, vector, weight = P("section", "dp", None), P("section", "dp"), P("section", "dp", None)
    out_specs = (
        tokens,
        tokens,
        vector,
        vector,
        weight,
        weight,
        vector,
        vector,
        vector,
        vector,
        weight,
        vector,
        weight,
        vector,
        vector,
        P("section", None, None, None),
    )
    return jax.shard_map(body, mesh=mesh, in_specs=in_specs, out_specs=out_specs, check_vma=False)
```

```python
import functools
import math

import jax
import jax.numpy as jnp
from jax import lax
from jax.experimental import pallas as pl
from jax.experimental.pallas import tpu as pltpu
from jax.sharding import PartitionSpec as P

D = 768
HEADS = 12
HEAD = 64
FF = 3072
RMAX = 15
NR = 31
SEQ = 64
ROWS = 128
BLOCK = 8
GROUP = 4 * HEAD
GROUPS = D // GROUP
TILE = 768
STEP = 32
BATCH = 2
FINE = 256
TILES = FF // TILE
SEL = D // BLOCK
SELP = SEL + 16
SELF = FF // BLOCK

EPSILON = 1e-06
FLOPS = 1000
MASKED = -1e30
C0 = math.sqrt(2.0 / math.pi)
C1 = C0 * 0.044715
F32 = jnp.float32
BF16 = jnp.bfloat16


def dot(left, right):
    return lax.dot_general(left, right, (((1,), (0,)), ((), ())), preferred_element_type=F32)


def dot_rt(left, right):
    return lax.dot_general(left, right, (((1,), (1,)), ((), ())), preferred_element_type=F32)


def dot_lt(left, right):
    return lax.dot_general(left, right, (((0,), (0,)), ((), ())), preferred_element_type=F32)


def normalize(rows):
    shifted = rows - jnp.mean(rows, axis=-1, keepdims=True)
    inverse = lax.rsqrt(jnp.mean(shifted * shifted, axis=-1, keepdims=True) + EPSILON)
    return shifted * inverse, inverse


def normalize_back(grad, normal, inverse):
    mean_grad = jnp.mean(grad, axis=-1, keepdims=True)
    mean_both = jnp.mean(grad * normal, axis=-1, keepdims=True)
    return (grad - mean_grad - normal * mean_both) * inverse


def column_sum(rows):
    return jnp.sum(rows, axis=0, keepdims=True)


def prepare_kernel(seg, cols, patches, cotangent, *refs):
    vectors, (out, vecs) = refs[:-2], refs[-2:]
    section = lax.axis_index("section")
    out[:ROWS, :] = jnp.where(section == 0, patches[...].astype(F32), cotangent[...].astype(F32))
    for k, vector in enumerate(vectors[:-1]):
        vecs[k : k + 1, :] = vector[...]
    for k in range(FF // D):
        vecs[8 + k : 9 + k, :] = vectors[-1][:, k * D : (k + 1) * D]
    segment = seg[...]
    lane = lax.broadcasted_iota(jnp.int32, (1, ROWS), 1)
    place = (lane % SEQ).astype(F32)
    second = lane >= SEQ
    start = jnp.zeros((1, ROWS), F32)
    width = jnp.zeros((1, ROWS), F32)
    before_first = jnp.zeros((1, 1), F32)
    before_second = jnp.zeros((1, 1), F32)
    for page in range(cols.shape[1]):
        member = segment == page
        ones = member.astype(F32)
        start += jnp.where(member, jnp.where(second, before_second, before_first), 0.0)
        width += jnp.where(member, jnp.where(second, cols[1, page], cols[0, page]).astype(F32), 0.0)
        before_first += jnp.sum(jnp.where(second, 0.0, ones), axis=1, keepdims=True)
        before_second += jnp.sum(jnp.where(second, ones, 0.0), axis=1, keepdims=True)
    width = jnp.maximum(width, 1.0)
    offset = place - start
    grid_row = jnp.floor((offset + 0.5) / width)
    grid_col = offset - grid_row * width
    line = lax.broadcasted_iota(jnp.int32, (8, ROWS), 0)
    out[ROWS:, :] = jnp.zeros((8, D), F32)
    out[ROWS:, :ROWS] = jnp.where(
        line == 0, segment.astype(F32), jnp.where(line == 1, grid_row, grid_col)
    )


def steps_of(meta, part):
    shape = (SEQ, ROWS)
    lane = lax.broadcasted_iota(jnp.int32, shape, 1)
    line = lax.broadcasted_iota(jnp.int32, shape, 0)
    left = lane < SEQ

    def across(values):
        wide = jnp.broadcast_to(values, (8, ROWS))
        swapped = pltpu.roll(wide, SEQ, 1)
        low = lax.broadcasted_iota(jnp.int32, (8, ROWS), 1) < SEQ
        both = jnp.where(low, wide, swapped) if part == 0 else jnp.where(low, swapped, wide)
        return both[:1]

    def down(values):
        return jnp.broadcast_to(values, (ROWS, ROWS)).T[part * SEQ : (part + 1) * SEQ, :]

    seg_i, row_i, col_i = (across(meta[k : k + 1]) for k in range(3))
    seg_j, row_j, col_j = (down(meta[k : k + 1]) for k in range(3))
    allowed = ((seg_i == seg_j) & (seg_j >= 0.0)) | ((lane % SEQ) == line)
    base = jnp.where(left, RMAX, RMAX + SEQ)
    row_step = jnp.clip(row_i - row_j, -RMAX, RMAX).astype(jnp.int32) + base
    col_step = jnp.clip(col_i - col_j, -RMAX, RMAX).astype(jnp.int32) + base
    return row_step, col_step, allowed


def fill_bias(meta, tabs, bias, first, part):
    if True:
        row_step, col_step, allowed = steps_of(meta, part)
        for pair in range(HEADS // 2):
            by_row = jnp.broadcast_to(tabs[pair : pair + 1, :], (SEQ, ROWS))
            by_col = jnp.broadcast_to(tabs[6 + pair : 7 + pair, :], (SEQ, ROWS))
            both = jnp.take_along_axis(by_row, row_step, axis=1) + jnp.take_along_axis(
                by_col, col_step, axis=1
            )
            bias[first + part, :, pair * ROWS : (pair + 1) * ROWS] = jnp.where(allowed, both, MASKED)


def diagonal_mask():
    line = lax.broadcasted_iota(jnp.int32, (GROUP, GROUP), 0) // HEAD
    lane = lax.broadcasted_iota(jnp.int32, (GROUP, GROUP), 1) // HEAD
    return line == lane


def spread(block, mask):
    return jnp.where(mask, jnp.concatenate([block] * 4, axis=0), jnp.zeros((), block.dtype))


def gather_diagonal(full):
    lane = lax.broadcasted_iota(jnp.int32, (SEQ, GROUP), 1) // HEAD
    result = full[:SEQ]
    for head in range(1, 4):
        result = jnp.where(lane == head, full[head * SEQ : (head + 1) * SEQ], result)
    return result


class Row:
    def __init__(self, ref, k):
        self.ref, self.k = ref, k

    def __call__(self):
        return self.ref[self.k : self.k + 1, :]


SUM_NAMES = ("sum_u", "sum_d", "sum_o", "sum_q", "sum_v")
SUM_SHAPES = ((SELP, FF), (SELF, D), (SELP, D), (SELP, 3 * D), (8, D))
SAVED = ("slope", "normal2", "inverse2", "branch", "sel", "act_sel", "qkv", "probs")
PACK = (SEL // 2 + 8, 4 * D + 3 * D + D + 4 * D)


class Scratch:
    def __init__(self, kind, shards):
        rows, seqs = shards * ROWS, 2 * shards
        spec = {
            "vecs": ((8 + FF // D, D), F32),
            "tabs": ((HEADS, 2 * SEQ), F32),
            "wq": ((D, 3 * D), BF16),
            "wo": ((D, D), BF16),
            "wu": ((D, FF), BF16),
            "x": ((rows, D), F32),
            "meta": ((shards, 8, ROWS), F32),
            "normed": ((rows, D), BF16),
            "qkv": ((rows, 3 * D), BF16),
            "bias": ((seqs, SEQ, D), F32),
            "probs": ((seqs, SEQ, D), BF16),
            "mixed": ((rows, D), BF16),
            "branch": ((rows, D), F32),
            "normal2": ((rows, D), F32),
            "inverse2": ((rows, ROWS), F32),
            "n2b": ((rows, D), BF16),
            "act": ((rows, FF), BF16),
            "slope": ((rows, FF), BF16),
        }
        if kind != "save":
            spec["wd"] = ((FF, D), BF16)
        if kind in ("save", "chunk"):
            spec["act_sel"] = ((rows, SELF), BF16)
            spec["sel"] = ((3, SELP, rows), BF16)
        if kind in ("fwd", "own"):
            spec["middle"] = ((ROWS, D), F32)
            spec["y"] = ((ROWS, D), F32)
        if kind != "save":
            spec["output"] = ((ROWS, D), F32)
        if kind in ("own", "chunk"):
            spec.update(
                parts=((8, D), F32),
                ds=((2, SEQ, D), BF16),
                u=((rows, D), F32),
                dob=((rows, D), BF16),
                dn2=((rows, D), F32),
                dbr=((rows, D), BF16),
                dmix=((rows, D), BF16),
                dqkv=((rows, 3 * D), BF16),
                dhid=((rows, FF), BF16),
                grad=((ROWS, D), F32),
            )
        if kind == "chunk":
            spec.update(zip(SUM_NAMES, ((shape, F32) for shape in SUM_SHAPES)))
            spec["small"] = ((24, D), F32)
        self.names = list(spec)
        self.shapes = [pltpu.VMEM(*spec[name]) for name in spec]

    def bind(self, refs):
        for name, ref in zip(self.names, refs):
            setattr(self, name, ref)
        return self


def saved_shapes(shards):
    scratch = Scratch("save", shards)
    shapes = dict(zip(scratch.names, scratch.shapes))
    return [jax.ShapeDtypeStruct(shapes[name].shape, shapes[name].dtype) for name in SAVED]


def layer_kernel(kind, shards, extras, first, last, *refs):
    refs = list(refs)

    def take(count):
        taken = refs[:count]
        del refs[:count]
        return taken

    rows = shards * ROWS
    seqs = 2 * shards
    vecs, tabs = take(2)
    wq, wo, wu, wd = take(4)
    a_refs = take(shards)
    b_refs = take(shards) if kind in ("own", "chunk") else []
    saved = take(len(SAVED)) if kind == "chunk" else []
    (output_in,) = take(1) if extras else (None,)
    (small_in,) = take(1) if last else (None,)
    sums_in = take(5) if kind == "chunk" and not first else []
    outs = {}
    if kind == "fwd":
        outs = dict(zip(("y", "output"), take(2)))
    elif kind == "own":
        outs = dict(zip(("y", "grad", "parts", "ds"), take(4)))
    elif kind == "save":
        outs = dict(zip(SAVED, take(len(SAVED))))
    elif last:
        packs = take(2)
    else:
        outs = dict(zip(SUM_NAMES, take(5)))
    if extras:
        outs.update(zip(("grad", "parts", "ds"), take(3)))
    scratch = Scratch(kind, shards)
    v = scratch.bind(take(len(scratch.names)))
    (sems,) = take(1)
    section = lax.axis_index("section")
    gain1, bias1, out_bias, attn_scale, gain2, bias2, down_bias, mlp_scale = (
        Row(v.vecs, k) for k in range(8)
    )
    index = {}
    tiles = [slice(k * TILE, (k + 1) * TILE) for k in range(TILES)]
    thirds = [slice(k * D, (k + 1) * D) for k in range(3)]
    shard_rows = [slice(k * ROWS, (k + 1) * ROWS) for k in range(shards)]
    table = {"vecs": (vecs, v.vecs), "tabs": (tabs, v.tabs), "wo": (wo, v.wo)}
    for k, span in enumerate(thirds):
        table[f"wq{k}"] = (wq.at[:, span], v.wq.at[:, span])
    for k, span in enumerate(tiles):
        table[f"wu{k}"] = (wu.at[:, span], v.wu.at[:, span])
        if kind != "save":
            table[f"wd{k}"] = (wd.at[span, :], v.wd.at[span, :])
    for k, span in enumerate(shard_rows):
        table[f"a{k}"] = (a_refs[k].at[:ROWS, :], v.x.at[span, :])
        table[f"meta{k}"] = (a_refs[k].at[ROWS : ROWS + 8, :ROWS], v.meta.at[k])
        if kind in ("own", "chunk"):
            table[f"u_a{k}"] = (a_refs[k].at[:ROWS, :], v.u.at[span, :])
            table[f"u_b{k}"] = (b_refs[k], v.u.at[span, :])
            table[f"b{k}"] = (b_refs[k], v.x.at[span, :])
    for k, ref in enumerate(saved):
        table["in_" + SAVED[k]] = (ref, getattr(v, SAVED[k]))
    for k, ref in enumerate(sums_in):
        table["in_" + SUM_NAMES[k]] = (ref, getattr(v, SUM_NAMES[k]))
    if extras:
        table["in_output"] = (output_in, v.output)
    if last:
        table["in_small"] = (small_in, v.small)
    for name, ref in outs.items():
        if name == "slope" or name == "qkv":
            for k, span in enumerate(tiles if name == "slope" else thirds):
                table[f"out_{name}{k}"] = (getattr(v, name).at[:, span], ref.at[:, span])
        else:
            table["out_" + name] = (getattr(v, name), ref)
    in_x = [f"a{k}" for k in range(shards)]
    in_meta = [f"meta{k}" for k in range(shards)]
    in_wq = ["wq0", "wq1", "wq2"]
    in_wu = [f"wu{k}" for k in range(TILES)]
    in_wd = [f"wd{k}" for k in range(TILES)]
    in_sums = ["in_" + name for name in SUM_NAMES] if sums_in else []
    stores = []

    def descriptor(name):
        source, target = table[name]
        return pltpu.make_async_copy(source, target, sems.at[index.setdefault(name, len(index))])

    def start(*names):
        for name in names:
            descriptor(name).start()

    def wait(*names):
        for name in names:
            descriptor(name).wait()

    def store(*names):
        start(*names)
        stores.extend(names)

    def blocks(count=shards):
        for first_row in range(0, count * ROWS, STEP):
            yield slice(first_row, first_row + STEP)

    def fold(total, values):
        for first_row in range(0, STEP, 8):
            total = total + values[first_row : first_row + 8]
        return total

    def pipelined(items, *stages):
        held = {}
        for k in range(len(items) + len(stages) - 1):
            for depth, stage in enumerate(stages):
                if 0 <= k - depth < len(items):
                    item = items[k - depth]
                    held[k - depth] = stage(item, held.get(k - depth))

    def centre(values):
        return values - jnp.mean(values, axis=-1, keepdims=True)

    def inverse_of(shifted):
        return lax.rsqrt(jnp.mean(shifted * shifted, axis=-1, keepdims=True) + EPSILON)

    def forward(x_names):
        wait("vecs", "tabs", *x_names, *in_meta)
        def norm_store(span, held):
            shifted, inverse = held
            v.normed[span, :] = (shifted * inverse * gain1() + bias1()).astype(BF16)

        pipelined(
            list(blocks()),
            lambda span, _: centre(v.x[span, :]),
            lambda span, shifted: (shifted, inverse_of(shifted)),
            norm_store,
        )
        wait(*in_wq)
        fill = [(shard, half) for shard in range(shards) for half in range(2)]
        for k, cols in enumerate(thirds):
            v.qkv[:, cols] = dot(v.normed[...], v.wq[:, cols]).astype(BF16)
            for shard, half in fill[k * len(fill) // 3 : (k + 1) * len(fill) // 3]:
                fill_bias(v.meta[shard], v.tabs, v.bias, 2 * shard, half)
        if kind == "save":
            store(*(f"out_qkv{k}" for k in range(3)))
        mask = diagonal_mask()
        units = [(s, g) for s in range(seqs) for g in range(GROUPS)]

        def score(unit):
            s, g = unit
            span, cols = slice(s * SEQ, (s + 1) * SEQ), slice(g * GROUP, (g + 1) * GROUP)
            query = v.qkv[span, cols] * BF16(0.125)
            key = v.qkv[span, D + g * GROUP : D + (g + 1) * GROUP]
            return dot_rt(key, spread(query, mask)) + v.bias[s, :, cols]

        def soften(unit, scores):
            s, g = unit
            grown = jnp.exp(scores - jnp.max(scores, axis=0, keepdims=True))
            prob = (grown * (1.0 / jnp.sum(grown, axis=0, keepdims=True))).astype(BF16)
            if kind != "fwd":
                v.probs[s, :, g * GROUP : (g + 1) * GROUP] = prob
            return prob

        def mix(unit, prob):
            s, g = unit
            span, cols = slice(s * SEQ, (s + 1) * SEQ), slice(g * GROUP, (g + 1) * GROUP)
            value = v.qkv[span, 2 * D + g * GROUP : 2 * D + (g + 1) * GROUP]
            v.mixed[span, cols] = gather_diagonal(dot_lt(prob, value)).astype(BF16)

        batches = [units[k : k + 2] for k in range(0, len(units), BATCH)]
        waiting_scores, waiting_probs = {}, {}
        for k in range(len(batches) + 2):
            if k < len(batches):
                waiting_scores[k] = [score(unit) for unit in batches[k]]
            if 0 <= k - 1 < len(batches):
                pairs = zip(batches[k - 1], waiting_scores.pop(k - 1))
                waiting_probs[k - 1] = [soften(unit, scores) for unit, scores in pairs]
            if 0 <= k - 2 < len(batches):
                for unit, prob in zip(batches[k - 2], waiting_probs.pop(k - 2)):
                    mix(unit, prob)

        if kind == "save":
            store("out_probs")
        wait("wo")
        v.branch[...] = dot(v.mixed[...], v.wo[...])
        def middle_of(span, _):
            branch_value = v.branch[span, :] + out_bias()
            v.branch[span, :] = branch_value
            middle_value = v.x[span, :] + attn_scale() * branch_value
            if kind in ("fwd", "own"):
                v.middle[span, :] = middle_value
            return centre(middle_value)

        def norm2_store(span, held):
            shifted, inverse = held
            normal2 = shifted * inverse
            if kind != "fwd":
                v.normal2[span, :] = normal2
                v.inverse2[span, :] = jnp.broadcast_to(inverse, (STEP, ROWS))
            v.n2b[span, :] = (normal2 * gain2() + bias2()).astype(BF16)

        pipelined(
            list(blocks()),
            middle_of,
            lambda span, shifted: (shifted, inverse_of(shifted)),
            norm2_store,
        )
        if kind == "save":
            store("out_normal2", "out_inverse2", "out_branch")
        wait(*in_wu)

        def hidden_of(low):
            return dot(v.n2b[...], v.wu[:, low : low + FINE])

        def activate(low, hidden):
            row, lane = 8 + low // D, low % D
            hidden = (hidden + v.vecs[row : row + 1, lane : lane + FINE]).astype(BF16)
            square = hidden * hidden
            share = 0.5 + 0.5 * jnp.tanh(hidden * (C0 + C1 * square))
            active = hidden * share
            v.act[:, low : low + FINE] = active.astype(BF16)
            if kind != "fwd":
                slope = share + active * (1.0 - share) * (2.0 * C0 + 6.0 * C1 * square)
                v.slope[:, low : low + FINE] = slope.astype(BF16)

        held = hidden_of(0)
        for low in range(0, FF, FINE):
            ahead = hidden_of(low + FINE) if low + FINE < FF else None
            activate(low, held)
            held = ahead
        if kind == "save":
            store(*(f"out_slope{k}" for k in range(TILES)))
        if kind in ("save", "chunk"):
            place = lax.axis_index("dp") // (lax.axis_size("dp") // BLOCK)
            line = lax.broadcasted_iota(jnp.int32, (SEL, D), 0)
            lane = lax.broadcasted_iota(jnp.int32, (SEL, D), 1)
            pick = (lane == line + place * SEL).astype(BF16)
            for k, source in enumerate((v.normed, v.mixed, v.n2b)):
                v.sel[k, :SEL] = dot_rt(pick, source[...]).astype(BF16)
                v.sel[k, SEL:] = jnp.ones((SELP - SEL, rows), BF16)
            v.act_sel[...] = v.act[:, pl.ds(pl.multiple_of(place * SELF, ROWS), SELF)]
        if kind == "save":
            store("out_sel", "out_act_sel")

    def backward_hidden():
        total_out = jnp.zeros((8, D), F32)
        for span in blocks():
            d_output = (mlp_scale() * v.u[span, :]).astype(BF16)
            v.dob[span, :] = d_output
            total_out = fold(total_out, d_output.astype(F32))
        wait(*in_wd)

        def slide(low, d_act):
            fine = slice(low, low + FINE)
            v.dhid[:, fine] = d_act.astype(BF16) * v.slope[:, fine]

        pipelined(
            list(range(0, FF, FINE)),
            lambda low, _: dot_rt(v.dob[...], v.wd[low : low + FINE, :]),
            slide,
        )
        return total_out

    def backward_middle():
        v.dn2[...] = dot_rt(v.dhid[...], v.wu[...])
        totals = [jnp.zeros((8, D), F32)] * 3

        def means(span, _):
            normal2 = v.normal2[span, :]
            grad = v.dn2[span, :] * gain2()
            mean_grad = jnp.mean(grad, axis=-1, keepdims=True)
            return mean_grad, jnp.mean(grad * normal2, axis=-1, keepdims=True)

        def finish(span, held):
            mean_grad, mean_both = held
            normal2, d_n2 = v.normal2[span, :], v.dn2[span, :]
            inverse2 = v.inverse2[span, :1]
            back = (d_n2 * gain2() - mean_grad - normal2 * mean_both) * inverse2
            d_middle = v.u[span, :] + back
            v.dbr[span, :] = (attn_scale() * d_middle).astype(BF16)
            if (kind == "own" or extras) and span.start < ROWS:
                v.grad[span, :] = d_middle
            if kind == "chunk":
                terms = (d_n2 * normal2, d_n2, d_middle * v.branch[span, :])
                totals[:] = [fold(total, term) for total, term in zip(totals, terms)]

        pipelined(list(blocks()), means, finish)
        return totals

    def backward_attention():
        v.dmix[...] = dot_rt(v.dbr[...], v.wo[...]).astype(BF16)
        mask = diagonal_mask()
        units = [(s, g) for s in range(seqs) for g in range(GROUPS)]
        batches = [units[k : k + BATCH] for k in range(0, len(units), BATCH)]

        def where_of(unit):
            s, g = unit
            return slice(s * SEQ, (s + 1) * SEQ), [
                slice(k * D + g * GROUP, k * D + (g + 1) * GROUP) for k in range(3)
            ]

        def probs_back(batch, _):
            made = []
            for unit in batch:
                span, cols = where_of(unit)
                d_mix = spread(v.dmix[span, cols[0]], mask)
                made.append((dot_rt(v.qkv[span, cols[2]], d_mix), d_mix))
            return made

        def scores_back(batch, held):
            made = []
            for unit, (d_prob, d_mix) in zip(batch, held):
                _, cols = where_of(unit)
                prob = v.probs[unit[0], :, cols[0]]
                wide = prob.astype(F32)
                delta = jnp.sum(wide * d_prob, axis=0, keepdims=True)
                d_score = (wide * (d_prob - delta)).astype(BF16)
                if kind == "own" or extras and unit[0] < 2:
                    v.ds[unit[0], :, cols[0]] = d_score
                made.append((d_score, prob, d_mix))
            return made

        def inputs_back(batch, held):
            for unit, (d_score, prob, d_mix) in zip(batch, held):
                span, cols = where_of(unit)
                query = spread(v.qkv[span, cols[0]] * BF16(0.125), mask)
                d_query = gather_diagonal(dot_lt(d_score, v.qkv[span, cols[1]])) * 0.125
                v.dqkv[span, cols[0]] = d_query.astype(BF16)
                v.dqkv[span, cols[1]] = dot(d_score, query).astype(BF16)
                v.dqkv[span, cols[2]] = dot(prob, d_mix).astype(BF16)

        pipelined(batches, probs_back, scores_back, inputs_back)

    def own_extras():
        v.dn2[:ROWS, :] = dot_rt(v.dqkv[:ROWS, :], v.wq[...])
        totals = [jnp.zeros((8, D), F32)] * 3
        for span in blocks(1):
            d_normed = v.dn2[span, :]
            normal, inverse = normalize(v.x[span, :])
            terms = (v.u[span, :] * v.output[span, :], d_normed * normal, d_normed)
            totals = [fold(total, term) for total, term in zip(totals, terms)]
            v.grad[span, :] += normalize_back(d_normed * gain1(), normal, inverse)
        for k in range(3):
            v.parts[k : k + 1, :] = column_sum(totals[k])

    def finish_layer():
        output = dot(v.act[...], v.wd[...]) + down_bias()
        v.output[...] = output
        v.y[...] = v.middle[...] + mlp_scale() * output

    def run_forward_only():
        start("vecs", "tabs", *in_x, *in_meta, *in_wq, "wo", *in_wu)
        if kind == "fwd":
            start(*in_wd)
        forward(in_x)
        if kind == "fwd":
            wait(*in_wd)
            finish_layer()
            store("out_y", "out_output")
        wait(*stores)

    def run_own():
        start("vecs", "tabs", "b0", "meta0", *in_wq, "wo", *in_wu, "u_a0", *in_wd)
        forward(["b0"])
        wait("u_a0")
        backward_hidden()
        finish_layer()
        store("out_y")
        backward_middle()
        backward_attention()
        store("out_ds")
        own_extras()
        store("out_grad", "out_parts")
        wait(*stores)

    def run_chunk():
        u_a, u_b = ([f"u_{side}{k}" for k in range(shards)] for side in "ab")
        in_b = [f"b{k}" for k in range(shards)]
        early = ["vecs", *u_b, "in_slope"]
        middle = [*in_wu, "in_normal2", "in_inverse2", "in_branch", "in_sel", "in_act_sel"]
        late = ["wo", "in_qkv", "in_probs"]
        own = ["a0", "in_output", *in_wq] if extras else []
        also = ["in_small"] if last else []

        @pl.when(section == 0)
        def _():
            start(*early, *in_wd, *middle, *in_sums, *late, *own, *also)
            wait(*early)

        @pl.when(section == 1)
        def _():
            start("vecs", "tabs", *in_b, *in_meta, *in_wq, "wo", *in_wu)
            start(*u_a, *in_wd, *in_sums, *also)
            forward(in_b)
            wait(*u_a)

        total_out = backward_hidden()

        @pl.when(section == 0)
        def _():
            wait(*middle)

        wait(*in_sums)

        def add(name, where, value):
            ref = getattr(v, name)
            ref[where] = value if first else ref[where] + value

        everything = (slice(None), slice(None))
        add("sum_u", everything, dot(v.sel[2], v.dhid[...]))
        add("sum_d", everything, dot_lt(v.act_sel[...], v.dob[...]))
        if last:
            pack_rows(0)
        else:
            store("out_sum_u", "out_sum_d")
        totals = [total_out] + backward_middle()
        for k, total in enumerate(totals):
            add("sum_v", (slice(k, k + 1), slice(None)), column_sum(total))
        add("sum_o", everything, dot(v.sel[1], v.dbr[...]))
        if last:
            wait(*also)
            pack_rows(1)
        else:
            store("out_sum_o", "out_sum_v")

        @pl.when(section == 0)
        def _():
            wait(*late)

        backward_attention()
        add("sum_q", everything, dot(v.sel[0], v.dqkv[...]))
        if last:
            pack_rows(2)
        else:
            store("out_sum_q")
        if extras:

            @pl.when(section == 0)
            def _():
                wait(*own)
                own_extras()
                start("out_grad", "out_parts", "out_ds")
                wait("out_grad", "out_parts", "out_ds")

        wait(*stores)

    def pack_rows(stage):
        core = lax.axis_index("dp") % 2
        half, quarter = SEL // 2, SELF // 8
        for side, target in enumerate(packs):
            whose = core if side == 0 else 1 - core
            low = pl.ds(pl.multiple_of(whose * half, 8), half)
            pieces = {}
            if stage == 0:
                pieces["u"] = (v.sum_u.at[low, :], target.at[:half, : 4 * D])
                for k in range(4):
                    start_row = pl.multiple_of(whose * (SELF // 2) + k * quarter, 8)
                    span = slice((8 + k) * D, (9 + k) * D)
                    piece = v.sum_d.at[pl.ds(start_row, quarter), :]
                    pieces[f"d{k}"] = (piece, target.at[:half, span])
            elif stage == 1:
                pieces["o"] = (v.sum_o.at[low, :], target.at[:half, 7 * D : 8 * D])
                tails = [v.sum_v.at[...], v.sum_o.at[SEL : SEL + 8, :]]
                tails += [v.sum_u.at[SEL : SEL + 8, k * D : (k + 1) * D] for k in range(FF // D)]
                tails += [v.small.at[8 * k : 8 * k + 8, :] for k in range(3)]
                for k, piece in enumerate(tails):
                    pieces[f"t{k}"] = (piece, target.at[half:, k * D : (k + 1) * D])
            else:
                pieces["q"] = (v.sum_q.at[low, :], target.at[:half, 4 * D : 7 * D])
            for name, piece in pieces.items():
                table[f"pack{side}{name}"] = piece
                store(f"pack{side}{name}")

    if kind in ("fwd", "save"):
        pl.when(section == 0)(run_forward_only)
    elif kind == "own":
        pl.when(section == 1)(run_own)
    else:
        run_chunk()


def run_layer(
    kind, vecs, tabs, weights, a_shards, b_shards=(), saved=(), output=None, sums=None, small=None
):
    shards = len(a_shards)
    hbm = pl.BlockSpec(memory_space=pl.ANY)
    extras, first, last = output is not None, sums is None, small is not None
    ins = [vecs, tabs, *weights, *a_shards, *b_shards, *saved]
    aliases = {}
    row_shape = jax.ShapeDtypeStruct((ROWS, D), F32)
    part_shape = jax.ShapeDtypeStruct((8, D), F32)
    score_shape = jax.ShapeDtypeStruct((2, SEQ, D), BF16)
    if kind == "fwd":
        outs = [row_shape] * 2
    elif kind == "own":
        outs = [row_shape, row_shape, part_shape, score_shape]
    elif kind == "save":
        outs = saved_shapes(shards)
    else:
        if last:
            outs = [jax.ShapeDtypeStruct(PACK, F32)] * 2
            ins.append(small)
        else:
            outs = [jax.ShapeDtypeStruct(shape, F32) for shape in SUM_SHAPES]
        if extras:
            ins.append(output)
            outs += [row_shape, part_shape, score_shape]
        if not first:
            if not last:
                aliases = {len(ins) + k: k for k in range(5)}
            ins += list(sums)
    return pl.pallas_call(
        functools.partial(layer_kernel, kind, shards, extras, first, last),
        out_shape=tuple(outs),
        in_specs=[hbm] * len(ins),
        out_specs=(hbm,) * len(outs),
        scratch_shapes=[*Scratch(kind, shards).shapes, pltpu.SemaphoreType.DMA((96,))],
        input_output_aliases=aliases,
        compiler_params=pltpu.CompilerParams(vmem_limit_bytes=60 * 1024 * 1024),
        cost_estimate=pl.CostEstimate(flops=FLOPS, bytes_accessed=1000, transcendentals=0),
        name="layer_" + kind,
    )(*ins)


def table_kernel(own, y0, y1, grad0, grad1, ds0, ds1, part0, part1, out, y_out, grad_out, rows_of):
    section = lax.axis_index("section")

    @pl.when(section == 0)
    def _():
        y_out[0] = y0[...]
        grad_out[0] = grad0[...]

    @pl.when(section == 1)
    def _():
        y_out[0] = y1[...]
        grad_out[0] = grad1[...]

    out[...] = jnp.zeros(out.shape, F32)
    out[0:8, :] = jnp.where(section == 0, part0[...], part1[...])
    rows_of[...] = jnp.zeros(rows_of.shape, F32)
    meta = own[ROWS:, :ROWS]
    lane = lax.broadcasted_iota(jnp.int32, (SEQ, ROWS), 1)
    steps = [steps_of(meta, part) for part in range(2)]
    for pair in range(HEADS // 2):
        span = slice(pair * ROWS, (pair + 1) * ROWS)
        grads = [
            jnp.where(section == 0, ds0[part, :, span], ds1[part, :, span]).astype(F32)
            for part in range(2)
        ]
        for kind, low, high in ((0, 0, NR), (1, RMAX - 7, RMAX + 8)):
            for r in range(low, high):
                total = jnp.zeros((8, ROWS), F32)
                for part in range(2):
                    step = steps[part][kind] - jnp.where(lane < SEQ, 0, SEQ)
                    chosen = jnp.where(step == r, grads[part], 0.0)
                    for line in range(0, SEQ, 8):
                        total = total + chosen[line : line + 8]
                rows_of[32 * kind + r : 32 * kind + r + 1, span] = column_sum(total)
    line = lax.broadcasted_iota(jnp.int32, (16, D), 0)
    head = lax.broadcasted_iota(jnp.int32, (16, D), 1) // HEAD
    ones = (line == head).astype(F32)
    out[8:24, : 2 * 32] = lax.dot_general(
        ones,
        rows_of[...],
        (((1,), (1,)), ((), ())),
        precision=lax.Precision.HIGHEST,
        preferred_element_type=F32,
    )


def finish_kernel(kept, received, *outs):
    outs, (mine, other, sems) = outs[:-3], outs[-3:]
    grad_q, grad_o, grad_u, grad_d, grad_ub, grad_table, *vectors = outs
    half = SEL // 2
    spans = [slice(0, 4 * D), slice(4 * D, 8 * D), slice(8 * D, 12 * D)]
    copies = []
    for k, span in enumerate(spans):
        copies.append(
            [
                pltpu.make_async_copy(kept.at[:, span], mine.at[:, span], sems.at[2 * k]),
                pltpu.make_async_copy(received.at[:, span], other.at[:, span], sems.at[2 * k + 1]),
            ]
        )
        for one in copies[-1]:
            one.start()
    device = lax.axis_index("dp")

    def total(lines, lanes):
        return mine[lines, lanes] + other[lines, lanes]

    body_rows, tail_rows = slice(0, half), slice(half, half + 8)
    for one in copies[0]:
        one.wait()
    grad_u[0] = total(body_rows, spans[0])
    for one in copies[1]:
        one.wait()
    sums_low, sums_out = (total(tail_rows, slice(k * D, (k + 1) * D)) for k in range(2))
    sums_up = [total(tail_rows, slice((2 + k) * D, (3 + k) * D))[:1] for k in range(FF // D)]
    small = [total(tail_rows, slice((6 + k) * D, (7 + k) * D)) for k in range(2)]
    width = vectors[0].shape[1]
    sources = (
        (small[0], 1),
        (small[0], 2),
        (sums_out, 0),
        (sums_low, 3),
        (sums_low, 1),
        (sums_low, 2),
        (sums_low, 0),
        (small[0], 0),
    )
    for out, (source, line) in zip(vectors, sources):
        out[...] = pltpu.roll(source, D - device * width, 1)[line : line + 1, :width]
    wide = grad_ub.shape[1]
    first = device * wide
    row = sums_up[0]
    for k in range(1, FF // D):
        row = jnp.where(first // D == k, sums_up[k], row)
    turned = pltpu.roll(jnp.broadcast_to(row, (8, D)), D - first % D, 1)
    grad_ub[...] = turned[:1, :wide]
    grad_q[0] = total(body_rows, slice(4 * D, 7 * D))
    grad_o[0] = total(body_rows, slice(7 * D, 8 * D))
    for one in copies[2]:
        one.wait()
    heads_low, heads_high = small[1], total(tail_rows, slice(8 * D, 9 * D))
    for t in range(2):
        grad_table[0, t, 0:8, :] = heads_low[:, 32 * t : 32 * t + NR]
        grad_table[0, t, 8:12, :] = heads_high[: HEADS - 8, 32 * t : 32 * t + NR]
    for k in range(4):
        grad_d[0, k * half : (k + 1) * half, :] = total(
            body_rows, slice((8 + k) * D, (9 + k) * D)
        )


def body(
    patches,
    cotangent,
    seg_ids,
    grid_cols,
    norm_gain1,
    norm_bias1,
    qkv_weight,
    out_weight,
    out_bias,
    attn_scale,
    norm_gain2,
    norm_bias2,
    up_weight,
    up_bias,
    down_weight,
    down_bias,
    mlp_scale,
    rel_table,
):
    dp_count = lax.axis_size("dp")
    supers = dp_count // (2 * BLOCK)
    section = lax.axis_index("section")
    device = lax.axis_index("dp")
    core = device % 2
    smem = pl.BlockSpec(memory_space=pltpu.SMEM)

    def pairs(move):
        return [
            (2 * (b * supers + s) + c, 2 * (move(b) * supers + s) + c)
            for b in range(BLOCK)
            for s in range(supers)
            for c in range(2)
        ]

    def along(array, step):
        return lax.ppermute(array, "dp", pairs(lambda b: (b // 2 + step) % 4 * 2 + b % 2))

    def across(array):
        return lax.ppermute(array, "dp", pairs(lambda b: b ^ 1))

    def sibling(array):
        return lax.ppermute(array, "dp", [(d, d ^ 1) for d in range(dp_count)])

    vectors = (
        norm_gain1,
        norm_bias1,
        out_bias,
        attn_scale,
        norm_gain2,
        norm_bias2,
        down_bias,
        mlp_scale,
        up_bias,
    )
    block = pl.BlockSpec()
    own, vecs = pl.pallas_call(
        prepare_kernel,
        out_shape=(
            jax.ShapeDtypeStruct((ROWS + 8, D), F32),
            jax.ShapeDtypeStruct((8 + FF // D, D), F32),
        ),
        in_specs=[block, smem] + [block] * (2 + len(vectors)),
        out_specs=(block,) * 2,
        name="prepare",
    )(seg_ids.reshape(1, ROWS), grid_cols, patches, cotangent, *vectors)
    tabs = jnp.pad(rel_table[0], ((0, 0), (0, 0), (0, SEQ - rel_table.shape[3]))).reshape(
        HEADS, 2 * SEQ
    )
    weights = (qkv_weight[0], out_weight[0], up_weight[0], down_weight[0])

    def after(array, *others):
        return lax.optimization_barrier((array, *others))[0]

    def layer(kind, *rest, **named):
        return run_layer(kind, vecs, tabs, weights, *rest, **named)

    y0, output0 = layer("fwd", [own])
    x1 = lax.ppermute(y0, "section", [(0, 1)])
    sent_a = after(own, y0)
    a_y = across(sent_a)
    a_z = [along(sent_a, step) for step in (1, 3, 2)]
    y1, grad1, part1, ds1 = layer("own", [own], [x1])
    u0 = lax.ppermute(grad1, "section", [(1, 0)])
    kept = [layer("save", [after(own, grad1), a_y])]
    a_z = [after(piece, kept[0][0]) for piece in a_z]
    a_yz = [across(piece) for piece in a_z]
    kept.append(layer("save", a_z[:2]))
    b_own = jnp.where(section == 0, after(u0, kept[1][0]), x1)
    b_y = across(b_own)
    b_z = [along(b_own, step) for step in (1, 3, 2)]
    kept.append(layer("save", [after(a_z[2], b_own), a_yz[0]]))
    *sums, grad0, part0, ds0 = layer(
        "chunk", [own, a_y], [b_own, b_y], (after(kept[0][0], kept[2][0]), *kept[0][1:]), output0
    )
    b_z = [after(piece, sums[0]) for piece in b_z]
    b_yz = [across(piece) for piece in b_z]
    sums = layer("chunk", a_z[:2], b_z[:2], kept[1], None, sums)
    small, section_out, section_grad = pl.pallas_call(
        table_kernel,
        out_shape=(
            jax.ShapeDtypeStruct((24, D), F32),
            jax.ShapeDtypeStruct((1, ROWS, D), F32),
            jax.ShapeDtypeStruct((1, ROWS, D), F32),
        ),
        scratch_shapes=[pltpu.VMEM((64, D), F32)],
        name="table",
    )(own, y0, y1, after(grad0, sums[0]), grad1, ds0, ds1, part0, part1)

    def flipped(array, flip):
        return lax.ppermute(array, "dp", pairs(lambda b: b ^ flip))

    moved = flipped(small, 4)
    kept.append(layer("save", [a_yz[1], after(a_yz[2], small)]))
    small = small + after(moved, kept[3][0])
    moved = flipped(small, 2)
    sums = layer("chunk", [a_z[2], a_yz[0]], [b_z[2], after(b_yz[0], small)], kept[2], None, sums)
    small = small + after(moved, sums[0])
    small = small + flipped(small, 1)
    final = small if supers == 1 else None
    sums = layer("chunk", a_yz[1:], b_yz[1:], kept[3], None, sums, final)
    width = D // dp_count
    wide = FF // dp_count
    if supers == 1:
        mine, others = sums
        hbm = pl.BlockSpec(memory_space=pl.ANY)
        shapes = [(1, width, 3 * D), (1, width, D), (1, width, FF), (1, wide, D), (1, wide)]
        shapes += [(1, 2, HEADS, NR)] + [(1, width)] * 8
        grad_q, grad_o, grad_u, grad_d, grad_ub, grad_table, *vectors = pl.pallas_call(
            finish_kernel,
            out_shape=tuple(jax.ShapeDtypeStruct(shape, F32) for shape in shapes),
            in_specs=[hbm, hbm],
            scratch_shapes=[
                pltpu.VMEM(PACK, F32),
                pltpu.VMEM(PACK, F32),
                pltpu.SemaphoreType.DMA((6,)),
            ],
            compiler_params=pltpu.CompilerParams(vmem_limit_bytes=32 * 1024 * 1024),
            name="finish",
        )(mine, sibling(others))
    else:
        sum_u, sum_d, sum_o, sum_q, sum_v = sums
        sum_v = jnp.concatenate(
            [sum_v[:4], sum_o[SEL : SEL + 1], sum_u[SEL : SEL + 1].reshape(FF // D, D)], axis=0
        )

        def shifted(array, step):
            moves = [
                (2 * (b * supers + s) + c, 2 * (b * supers + (s + step) % supers) + c)
                for b in range(BLOCK)
                for s in range(supers)
                for c in range(2)
            ]
            return lax.ppermute(array, "dp", moves)

        def scatter(partial):
            parts = partial.reshape(supers, 2, partial.shape[0] // (2 * supers), partial.shape[1])
            held = lax.dynamic_index_in_dim(parts, core, 1, keepdims=False)
            held = held + sibling(lax.dynamic_index_in_dim(parts, 1 - core, 1, keepdims=False))
            place = device // 2 % supers
            total = lax.dynamic_index_in_dim(held, place, 0, keepdims=False)
            for step in range(1, supers):
                there = (place + step) % supers
                total = total + shifted(
                    lax.dynamic_index_in_dim(held, there, 0, keepdims=False), step
                )
            return total[None]

        sums = jnp.concatenate([sum_v, small[:8], small[8:]], axis=0)
        sums = sums + sibling(sums)
        sums = sums + sum(shifted(sums, step) for step in range(1, supers))
        vectors = [
            lax.dynamic_slice(sums, (row, device * width), (1, width))
            for row in (10, 11, 4, 3, 1, 2, 0, 9)
        ]
        grad_ub = lax.dynamic_slice(sums[5:9].reshape(1, FF), (0, device * wide), (1, wide))
        grad_table = sums[17 : 17 + HEADS, :64].reshape(HEADS, 2, 32)[:, :, :NR]
        grad_table = grad_table.transpose(1, 0, 2)[None]
        grad_q, grad_o, grad_u, grad_d = (
            scatter(partial) for partial in (sum_q[:SEL], sum_o[:SEL], sum_u[:SEL], sum_d)
        )
    gain1, bias1, out_b, attn, gain2, bias2, down_b, mlp = vectors
    return (
        section_out,
        section_grad,
        gain1,
        bias1,
        grad_q,
        grad_o,
        out_b,
        attn,
        gain2,
        bias2,
        grad_u,
        grad_ub,
        grad_d,
        down_b,
        mlp,
        grad_table,
    )


def solution(mesh):
    row, whole = P("dp", None), P("section", None)
    matrix = P("section", None, None)
    in_specs = (
        row,
        row,
        P("dp"),
        row,
        whole,
        whole,
        matrix,
        matrix,
        whole,
        whole,
        whole,
        whole,
        matrix,
        whole,
        matrix,
        whole,
        whole,
        P("section", None, None, None),
    )
    tokens, vector, weight = P("section", "dp", None), P("section", "dp"), P("section", "dp", None)
    out_specs = (
        tokens,
        tokens,
        vector,
        vector,
        weight,
        weight,
        vector,
        vector,
        vector,
        vector,
        weight,
        vector,
        weight,
        vector,
        vector,
        P("section", None, None, None),
    )
    return jax.shard_map(body, mesh=mesh, in_specs=in_specs, out_specs=out_specs, check_vma=False)
```

```python
import functools
import math

import jax
import jax.numpy as jnp
from jax import lax
from jax.experimental import pallas as pl
from jax.experimental.pallas import tpu as pltpu
from jax.sharding import PartitionSpec as P

D = 768
HEADS = 12
HEAD = 64
FF = 3072
RMAX = 15
NR = 31
SEQ = 64
ROWS = 128
BLOCK = 8
GROUP = 4 * HEAD
GROUPS = D // GROUP
TILE = 768
STEP = 32
BATCH = 6
AHEAD = 3
FINE = 256
TILES = FF // TILE
SEL = D // BLOCK
SELP = SEL + 16
SELF = FF // BLOCK

EPSILON = 1e-06
WORK = {"fwd": 1, "own": 1, "save": 1, "chunk": 1}
MASKED = -1e30
C0 = math.sqrt(2.0 / math.pi)
C1 = C0 * 0.044715
F32 = jnp.float32
BF16 = jnp.bfloat16


def dot(left, right):
    return lax.dot_general(left, right, (((1,), (0,)), ((), ())), preferred_element_type=F32)


def dot_rt(left, right):
    return lax.dot_general(left, right, (((1,), (1,)), ((), ())), preferred_element_type=F32)


def dot_lt(left, right):
    return lax.dot_general(left, right, (((0,), (0,)), ((), ())), preferred_element_type=F32)


def normalize(rows):
    shifted = rows - jnp.mean(rows, axis=-1, keepdims=True)
    inverse = lax.rsqrt(jnp.mean(shifted * shifted, axis=-1, keepdims=True) + EPSILON)
    return shifted * inverse, inverse


def normalize_back(grad, normal, inverse):
    mean_grad = jnp.mean(grad, axis=-1, keepdims=True)
    mean_both = jnp.mean(grad * normal, axis=-1, keepdims=True)
    return (grad - mean_grad - normal * mean_both) * inverse


def column_sum(rows):
    return jnp.sum(rows, axis=0, keepdims=True)


def grid_places(segment, cols):
    lane = lax.broadcasted_iota(jnp.int32, (1, ROWS), 1)
    place = (lane % SEQ).astype(F32)
    second = lane >= SEQ
    start = jnp.zeros((1, ROWS), F32)
    width = jnp.zeros((1, ROWS), F32)
    before_first = jnp.zeros((1, 1), F32)
    before_second = jnp.zeros((1, 1), F32)
    for page in range(cols.shape[1]):
        member = segment == page
        ones = member.astype(F32)
        start += jnp.where(member, jnp.where(second, before_second, before_first), 0.0)
        width += jnp.where(member, jnp.where(second, cols[1, page], cols[0, page]).astype(F32), 0.0)
        before_first += jnp.sum(jnp.where(second, 0.0, ones), axis=1, keepdims=True)
        before_second += jnp.sum(jnp.where(second, ones, 0.0), axis=1, keepdims=True)
    offset = place - start
    width = jnp.maximum(width, 1.0)
    grid_row = jnp.floor((offset + 0.5) / width)
    grid_col = offset - grid_row * width
    line = lax.broadcasted_iota(jnp.int32, (8, ROWS), 0)
    return jnp.where(
        line == 0, segment.astype(F32), jnp.where(line == 1, grid_row, grid_col)
    )


def steps_of(meta, part):
    shape = (SEQ, ROWS)
    lane = lax.broadcasted_iota(jnp.int32, shape, 1)
    line = lax.broadcasted_iota(jnp.int32, shape, 0)
    left = lane < SEQ

    def across(values):
        wide = jnp.broadcast_to(values, (8, ROWS))
        swapped = pltpu.roll(wide, SEQ, 1)
        low = lax.broadcasted_iota(jnp.int32, (8, ROWS), 1) < SEQ
        both = jnp.where(low, wide, swapped) if part == 0 else jnp.where(low, swapped, wide)
        return both[:1]

    def down(values):
        return jnp.broadcast_to(values, (ROWS, ROWS)).T[part * SEQ : (part + 1) * SEQ, :]

    seg_i, row_i, col_i = (across(meta[k : k + 1]) for k in range(3))
    seg_j, row_j, col_j = (down(meta[k : k + 1]) for k in range(3))
    allowed = ((seg_i == seg_j) & (seg_j >= 0.0)) | ((lane % SEQ) == line)
    base = jnp.where(left, RMAX, RMAX + SEQ)
    row_step = jnp.clip(row_i - row_j, -RMAX, RMAX).astype(jnp.int32) + base
    col_step = jnp.clip(col_i - col_j, -RMAX, RMAX).astype(jnp.int32) + base
    return row_step, col_step, allowed


def fill_bias(meta, tabs, bias, first, part):
    if True:
        row_step, col_step, allowed = steps_of(meta, part)
        for pair in range(HEADS // 2):
            by_row = jnp.broadcast_to(tabs[pair : pair + 1, :], (SEQ, ROWS))
            by_col = jnp.broadcast_to(tabs[6 + pair : 7 + pair, :], (SEQ, ROWS))
            both = jnp.take_along_axis(by_row, row_step, axis=1) + jnp.take_along_axis(
                by_col, col_step, axis=1
            )
            bias[first + part, :, pair * ROWS : (pair + 1) * ROWS] = jnp.where(allowed, both, MASKED)


def diagonal_mask():
    line = lax.broadcasted_iota(jnp.int32, (GROUP, GROUP), 0) // HEAD
    lane = lax.broadcasted_iota(jnp.int32, (GROUP, GROUP), 1) // HEAD
    return line == lane


def spread(block, mask):
    return jnp.where(mask, jnp.concatenate([block] * 4, axis=0), jnp.zeros((), block.dtype))


def gather_diagonal(full):
    lane = lax.broadcasted_iota(jnp.int32, (SEQ, GROUP), 1) // HEAD
    result = full[:SEQ]
    for head in range(1, 4):
        result = jnp.where(lane == head, full[head * SEQ : (head + 1) * SEQ], result)
    return result


class Row:
    def __init__(self, ref, k):
        self.ref, self.k = ref, k

    def __call__(self):
        return self.ref[self.k : self.k + 1, :]


SUM_NAMES = ("sum_u", "sum_d", "sum_o", "sum_q", "sum_v")
SUM_SHAPES = ((SELP, FF), (SELF, D), (SELP, D), (SELP, 3 * D), (8, D))
FIRST = ("segment", "rel", "patches", "cotangent", *(f"vector{k}" for k in range(8)), "up_bias")
SAVED = ("slope", "normal2", "inverse2", "branch", "sel", "act_sel", "qkv", "probs")
SHARED = {"a": "x", "b": "x", "u_a": "u", "u_b": "u"}
PACK = (SEL // 2 + 8, 4 * D + 3 * D + D + 4 * D)


class Scratch:
    def __init__(self, kind, shards):
        rows, seqs = shards * ROWS, 2 * shards
        spec = {
            "vecs": ((8 + FF // D, D), F32),
            "tabs": ((HEADS, 2 * SEQ), F32),
            "wq": ((D, 3 * D), BF16),
            "wo": ((D, D), BF16),
            "wu": ((D, FF), BF16),
            "x": ((rows, D), F32),
            "meta": ((shards, 8, ROWS), F32),
            "normed": ((rows, D), BF16),
            "qkv": ((rows, 3 * D), BF16),
            "bias": ((seqs, SEQ, D), F32),
            "probs": ((seqs, SEQ, D), BF16),
            "mixed": ((rows, D), BF16),
            "branch": ((rows, D), F32),
            "normal2": ((rows, D), F32),
            "inverse2": ((rows, ROWS), F32),
            "n2b": ((rows, D), BF16),
            "act": ((rows, FF), BF16),
            "slope": ((rows, FF), BF16),
        }
        if kind != "save":
            spec["wd"] = ((FF, D), BF16)
        if kind in ("save", "chunk"):
            spec["act_sel"] = ((rows, SELF), BF16)
            spec["sel"] = ((3, SELP, rows), BF16)
        if kind == "fwd":
            spec.update((f"vector{k}", ((1, D), F32)) for k in range(8))
            spec["up_bias"] = ((1, FF), F32)
            spec["segment"] = ((1, ROWS), jnp.int32)
            spec["rel"] = ((HEADS, 2, NR), F32)
            spec["patches"] = ((ROWS, D), BF16)
            spec["cotangent"] = ((ROWS, D), BF16)
            spec["payload"] = ((ROWS + 8, D), F32)
        if kind in ("fwd", "chunk"):
            spec["middle"] = ((ROWS, D), F32)
            spec["y"] = ((ROWS, D), F32)
            spec["output"] = ((ROWS, D), F32)
        if kind in ("own", "chunk"):
            spec.update(
                u=((rows, D), F32),
                dob=((rows, D), BF16),
                dn2=((rows, D), F32),
                dbr=((rows, D), BF16),
                dmix=((rows, D), BF16),
                dqkv=((rows, 3 * D), BF16),
                dhid=((rows, FF), BF16),
                grad=((ROWS, D), F32),
            )
        if kind == "chunk":
            spec.update(zip(SUM_NAMES, ((shape, F32) for shape in SUM_SHAPES)))
            spec["small"] = ((24, D), F32)
            spec["steps"] = ((64, D), F32)
            spec["ds"] = ((2, SEQ, D), BF16)
        self.names = list(spec)
        self.shapes = [pltpu.VMEM(*spec[name]) for name in spec]

    def bind(self, refs):
        for name, ref in zip(self.names, refs):
            setattr(self, name, ref)
        return self


def saved_shapes(shards):
    scratch = Scratch("save", shards)
    shapes = dict(zip(scratch.names, scratch.shapes))
    return [jax.ShapeDtypeStruct(shapes[name].shape, shapes[name].dtype) for name in SAVED]


def layer_kernel(kind, shards, split, extras, first, last, *refs):
    refs = list(refs)

    def take(count):
        taken = refs[:count]
        del refs[:count]
        return taken

    rows = shards * ROWS
    seqs = 2 * shards
    if kind == "fwd":
        cols, *first_ins = take(1 + len(FIRST))
    else:
        vecs, tabs = take(2)
    wq, wo, wu, wd = take(4)
    a_refs = take(shards) if kind != "fwd" else []
    b_refs = take(shards) if kind in ("own", "chunk") else []
    saved = take(len(SAVED)) if kind == "chunk" and split else []
    y_in, output_in = take(2) if extras else (None, None)
    sums_in = take(5) if kind == "chunk" and not first else []
    outs = {}
    if kind == "fwd":
        outs = dict(zip(("payload", "vecs", "tabs", "y", "output"), take(5)))
    elif kind == "own":
        outs = dict(zip(("grad",), take(1)))
    elif kind == "save":
        outs = dict(zip(SAVED, take(len(SAVED))))
    elif last:
        packs = take(2)
    else:
        outs = dict(zip(SUM_NAMES, take(5)))
    if extras:
        outs.update(zip(("y", "grad", "small"), take(3)))
    scratch = Scratch(kind, shards)
    v = scratch.bind(take(len(scratch.names)))
    (sems,) = take(1)
    section = lax.axis_index("section")
    gain1, bias1, out_bias, attn_scale, gain2, bias2, down_bias, mlp_scale = (
        Row(v.vecs, k) for k in range(8)
    )
    index = {}
    tiles = [slice(k * TILE, (k + 1) * TILE) for k in range(TILES)]
    thirds = [slice(k * D, (k + 1) * D) for k in range(3)]
    shard_rows = [slice(k * ROWS, (k + 1) * ROWS) for k in range(shards)]
    table = {"wo": (wo, v.wo)}
    if kind == "fwd":
        table.update((name, (ref, getattr(v, name))) for name, ref in zip(FIRST, first_ins))
    else:
        table.update(vecs=(vecs, v.vecs), tabs=(tabs, v.tabs))
    for k, span in enumerate(thirds):
        table[f"wq{k}"] = (wq.at[:, span], v.wq.at[:, span])
    for k, span in enumerate(tiles):
        table[f"wu{k}"] = (wu.at[:, span], v.wu.at[:, span])
        if kind != "save":
            table[f"wd{k}"] = (wd.at[span, :], v.wd.at[span, :])
    for k, span in enumerate(shard_rows if a_refs else []):
        table[f"a{k}"] = (a_refs[k].at[:ROWS, :], v.x.at[span, :])
        table[f"meta{k}"] = (a_refs[k].at[ROWS : ROWS + 8, :ROWS], v.meta.at[k])
        if kind in ("own", "chunk"):
            table[f"u_a{k}"] = (a_refs[k].at[:ROWS, :], v.u.at[span, :])
            table[f"u_b{k}"] = (b_refs[k], v.u.at[span, :])
            table[f"b{k}"] = (b_refs[k], v.x.at[span, :])
    for k, ref in enumerate(saved):
        table["in_" + SAVED[k]] = (ref, getattr(v, SAVED[k]))
    for k, ref in enumerate(sums_in):
        table["in_" + SUM_NAMES[k]] = (ref, getattr(v, SUM_NAMES[k]))
    if extras:
        table["in_y"] = (y_in, v.y)
        table["in_output"] = (output_in, v.output)
    for name, ref in outs.items():
        if name == "slope" or name == "qkv":
            for k, span in enumerate(tiles if name == "slope" else thirds):
                table[f"out_{name}{k}"] = (getattr(v, name).at[:, span], ref.at[:, span])
        else:
            target = ref.at[0] if extras and name in ("y", "grad") else ref
            table["out_" + name] = (getattr(v, name), target)
    in_x = [f"a{k}" for k in range(shards)]
    in_meta = [f"meta{k}" for k in range(shards)]
    in_wq = ["wq0", "wq1", "wq2"]
    in_wu = [f"wu{k}" for k in range(TILES)]
    in_wd = [f"wd{k}" for k in range(TILES)]
    in_sums = ["in_" + name for name in SUM_NAMES] if sums_in else []
    stores = []

    def descriptor(name):
        source, target = table[name]
        shared = SHARED.get(name[:-1], name[:-1]) + name[-1]
        return pltpu.make_async_copy(source, target, sems.at[index.setdefault(shared, len(index))])

    def start(*names):
        for name in names:
            descriptor(name).start()

    def wait(*names):
        for name in names:
            descriptor(name).wait()

    def store(*names):
        start(*names)
        stores.extend(names)

    def blocks(count=shards):
        for first_row in range(0, count * ROWS, STEP):
            yield slice(first_row, first_row + STEP)

    def fold(total, values):
        for first_row in range(0, STEP, 8):
            total = total + values[first_row : first_row + 8]
        return total

    def pipelined(items, *stages):
        held = {}
        for k in range(len(items) + len(stages) - 1):
            for depth, stage in enumerate(stages):
                if 0 <= k - depth < len(items):
                    item = items[k - depth]
                    held[k - depth] = stage(item, held.get(k - depth))

    def centre(values):
        return values - jnp.mean(values, axis=-1, keepdims=True)

    def inverse_of(shifted):
        return lax.rsqrt(jnp.mean(shifted * shifted, axis=-1, keepdims=True) + EPSILON)

    def forward(x_names):
        if kind != "fwd":
            wait("vecs", "tabs", *x_names, *in_meta)
        def norm_store(span, held):
            shifted, inverse = held
            v.normed[span, :] = (shifted * inverse * gain1() + bias1()).astype(BF16)

        pipelined(
            list(blocks()),
            lambda span, _: centre(v.x[span, :]),
            lambda span, shifted: (shifted, inverse_of(shifted)),
            norm_store,
        )
        wait(*in_wq)
        fill = [(shard, half) for shard in range(shards) for half in range(2)]
        for k, cols in enumerate(thirds):
            v.qkv[:, cols] = dot(v.normed[...], v.wq[:, cols]).astype(BF16)
            for shard, half in fill[k * len(fill) // 3 : (k + 1) * len(fill) // 3]:
                fill_bias(v.meta[shard], v.tabs, v.bias, 2 * shard, half)
        if kind == "save":
            store(*(f"out_qkv{k}" for k in range(3)))
        mask = diagonal_mask()
        units = [(s, g) for s in range(seqs) for g in range(GROUPS)]

        def score(unit):
            s, g = unit
            span, cols = slice(s * SEQ, (s + 1) * SEQ), slice(g * GROUP, (g + 1) * GROUP)
            query = v.qkv[span, cols] * BF16(0.125)
            key = v.qkv[span, D + g * GROUP : D + (g + 1) * GROUP]
            return dot_rt(key, spread(query, mask)) + v.bias[s, :, cols]

        def soften(unit, scores):
            s, g = unit
            grown = jnp.exp(scores - jnp.max(scores, axis=0, keepdims=True))
            prob = (grown * (1.0 / jnp.sum(grown, axis=0, keepdims=True))).astype(BF16)
            if kind != "fwd":
                v.probs[s, :, g * GROUP : (g + 1) * GROUP] = prob
            return prob

        def mix(unit, prob):
            s, g = unit
            span, cols = slice(s * SEQ, (s + 1) * SEQ), slice(g * GROUP, (g + 1) * GROUP)
            value = v.qkv[span, 2 * D + g * GROUP : 2 * D + (g + 1) * GROUP]
            v.mixed[span, cols] = gather_diagonal(dot_lt(prob, value)).astype(BF16)

        batches = [units[k : k + AHEAD] for k in range(0, len(units), AHEAD)]
        waiting_scores, waiting_probs = {}, {}
        for k in range(len(batches) + 2):
            if k < len(batches):
                waiting_scores[k] = [score(unit) for unit in batches[k]]
            if 0 <= k - 1 < len(batches):
                pairs = zip(batches[k - 1], waiting_scores.pop(k - 1))
                waiting_probs[k - 1] = [soften(unit, scores) for unit, scores in pairs]
            if 0 <= k - 2 < len(batches):
                for unit, prob in zip(batches[k - 2], waiting_probs.pop(k - 2)):
                    mix(unit, prob)

        if kind == "save":
            store("out_probs")
        wait("wo")
        v.branch[...] = dot(v.mixed[...], v.wo[...])
        def middle_of(span, _):
            branch_value = v.branch[span, :] + out_bias()
            v.branch[span, :] = branch_value
            middle_value = v.x[span, :] + attn_scale() * branch_value
            if (kind == "fwd" or extras) and span.start < ROWS:
                v.middle[span, :] = middle_value
            return centre(middle_value)

        def norm2_store(span, held):
            shifted, inverse = held
            normal2 = shifted * inverse
            if kind != "fwd":
                v.normal2[span, :] = normal2
                v.inverse2[span, :] = jnp.broadcast_to(inverse, (STEP, ROWS))
            v.n2b[span, :] = (normal2 * gain2() + bias2()).astype(BF16)

        pipelined(
            list(blocks()),
            middle_of,
            lambda span, shifted: (shifted, inverse_of(shifted)),
            norm2_store,
        )
        if kind == "save":
            store("out_normal2", "out_inverse2", "out_branch")
        wait(*in_wu)

        def hidden_of(low):
            return dot(v.n2b[...], v.wu[:, low : low + FINE])

        def activate(low, hidden):
            row, lane = 8 + low // D, low % D
            hidden = (hidden + v.vecs[row : row + 1, lane : lane + FINE]).astype(BF16)
            square = hidden * hidden
            share = 0.5 + 0.5 * jnp.tanh(hidden * (C0 + C1 * square))
            active = hidden * share
            v.act[:, low : low + FINE] = active.astype(BF16)
            if kind != "fwd":
                slope = share + active * (1.0 - share) * (2.0 * C0 + 6.0 * C1 * square)
                v.slope[:, low : low + FINE] = slope.astype(BF16)

        held = hidden_of(0)
        for low in range(0, FF, FINE):
            ahead = hidden_of(low + FINE) if low + FINE < FF else None
            activate(low, held)
            held = ahead
        if kind == "save":
            store(*(f"out_slope{k}" for k in range(TILES)))
        if kind in ("save", "chunk"):
            place = lax.axis_index("dp") // (lax.axis_size("dp") // BLOCK)
            line = lax.broadcasted_iota(jnp.int32, (SEL, D), 0)
            lane = lax.broadcasted_iota(jnp.int32, (SEL, D), 1)
            pick = (lane == line + place * SEL).astype(BF16)
            for k, source in enumerate((v.normed, v.mixed, v.n2b)):
                v.sel[k, :SEL] = dot_rt(pick, source[...]).astype(BF16)
                v.sel[k, SEL:] = jnp.ones((SELP - SEL, rows), BF16)
            v.act_sel[...] = v.act[:, pl.ds(pl.multiple_of(place * SELF, ROWS), SELF)]
        if kind == "save":
            store("out_sel", "out_act_sel")

    def backward_hidden():
        total_out = jnp.zeros((8, D), F32)
        for span in blocks():
            d_output = (mlp_scale() * v.u[span, :]).astype(BF16)
            v.dob[span, :] = d_output
            total_out = fold(total_out, d_output.astype(F32))
        if not split:
            wait(*in_wd)

        def slide(low, d_act):
            fine = slice(low, low + FINE)
            v.dhid[:, fine] = d_act.astype(BF16) * v.slope[:, fine]

        pipelined(
            list(range(0, FF, FINE)),
            lambda low, _: dot_rt(v.dob[...], v.wd[low : low + FINE, :]),
            slide,
        )
        return total_out

    def backward_middle():
        v.dn2[...] = dot_rt(v.dhid[...], v.wu[...])
        totals = [jnp.zeros((8, D), F32)] * 3

        def means(span, _):
            normal2 = v.normal2[span, :]
            grad = v.dn2[span, :] * gain2()
            mean_grad = jnp.mean(grad, axis=-1, keepdims=True)
            return mean_grad, jnp.mean(grad * normal2, axis=-1, keepdims=True)

        def finish(span, held):
            mean_grad, mean_both = held
            normal2, d_n2 = v.normal2[span, :], v.dn2[span, :]
            inverse2 = v.inverse2[span, :1]
            back = (d_n2 * gain2() - mean_grad - normal2 * mean_both) * inverse2
            d_middle = v.u[span, :] + back
            v.dbr[span, :] = (attn_scale() * d_middle).astype(BF16)
            if (kind == "own" or extras) and span.start < ROWS:
                v.grad[span, :] = d_middle
            if kind == "chunk":
                terms = (d_n2 * normal2, d_n2, d_middle * v.branch[span, :])
                totals[:] = [fold(total, term) for total, term in zip(totals, terms)]

        pipelined(list(blocks()), means, finish)
        return totals

    def backward_attention():
        v.dmix[...] = dot_rt(v.dbr[...], v.wo[...]).astype(BF16)
        mask = diagonal_mask()
        units = [(s, g) for s in range(seqs) for g in range(GROUPS)]
        batches = [units[k : k + BATCH] for k in range(0, len(units), BATCH)]

        def where_of(unit):
            s, g = unit
            return slice(s * SEQ, (s + 1) * SEQ), [
                slice(k * D + g * GROUP, k * D + (g + 1) * GROUP) for k in range(3)
            ]

        def probs_back(batch, _):
            made = []
            for unit in batch:
                span, cols = where_of(unit)
                d_mix = spread(v.dmix[span, cols[0]], mask)
                made.append((dot_rt(v.qkv[span, cols[2]], d_mix), d_mix))
            return made

        def scores_back(batch, held):
            made = []
            for unit, (d_prob, d_mix) in zip(batch, held):
                _, cols = where_of(unit)
                prob = v.probs[unit[0], :, cols[0]]
                wide = prob.astype(F32)
                delta = jnp.sum(wide * d_prob, axis=0, keepdims=True)
                d_score = (wide * (d_prob - delta)).astype(BF16)
                if extras and unit[0] < 2:
                    v.ds[unit[0], :, cols[0]] = d_score
                made.append((d_score, prob, d_mix))
            return made

        def inputs_back(batch, held):
            for unit, (d_score, prob, d_mix) in zip(batch, held):
                span, cols = where_of(unit)
                query = spread(v.qkv[span, cols[0]] * BF16(0.125), mask)
                d_query = gather_diagonal(dot_lt(d_score, v.qkv[span, cols[1]])) * 0.125
                v.dqkv[span, cols[0]] = d_query.astype(BF16)
                v.dqkv[span, cols[1]] = dot(d_score, query).astype(BF16)
                v.dqkv[span, cols[2]] = dot(prob, d_mix).astype(BF16)

        pipelined(batches, probs_back, scores_back, inputs_back)

    def own_input_grad():
        v.dn2[:ROWS, :] = dot_rt(v.dqkv[:ROWS, :], v.wq[...])
        totals = [jnp.zeros((8, D), F32)] * 3

        def finish(span, held):
            shifted, inverse = held
            d_normed, normal = v.dn2[span, :], shifted * inverse
            if extras:
                terms = (v.u[span, :] * v.output[span, :], d_normed * normal, d_normed)
                totals[:] = [fold(total, term) for total, term in zip(totals, terms)]
            v.grad[span, :] += normalize_back(d_normed * gain1(), normal, inverse)

        pipelined(
            list(blocks(1)),
            lambda span, _: centre(v.x[span, :]),
            lambda span, shifted: (shifted, inverse_of(shifted)),
            finish,
        )
        return totals

    def finish_layer():
        output = dot(v.act[:ROWS, :], v.wd[...]) + down_bias()
        v.output[...] = output
        v.y[...] = v.middle[...] + mlp_scale() * output

    def own_extras():
        totals = own_input_grad()
        v.small[...] = jnp.zeros((24, D), F32)
        for k in range(3):
            v.small[k : k + 1, :] = column_sum(totals[k])
        v.steps[...] = jnp.zeros((64, D), F32)
        lane = lax.broadcasted_iota(jnp.int32, (SEQ, ROWS), 1)
        steps = [steps_of(v.meta[0], half) for half in range(2)]
        for pair in range(HEADS // 2):
            span = slice(pair * ROWS, (pair + 1) * ROWS)
            grads = [v.ds[half, :, span].astype(F32) for half in range(2)]
            for which, low, high in ((0, 0, NR), (1, RMAX - 7, RMAX + 8)):
                for r in range(low, high):
                    total = jnp.zeros((8, ROWS), F32)
                    for half in range(2):
                        step = steps[half][which] - jnp.where(lane < SEQ, 0, SEQ)
                        chosen = jnp.where(step == r, grads[half], 0.0)
                        for line in range(0, SEQ, 8):
                            total = total + chosen[line : line + 8]
                    v.steps[32 * which + r : 32 * which + r + 1, span] = column_sum(total)
        line = lax.broadcasted_iota(jnp.int32, (16, D), 0)
        head = lax.broadcasted_iota(jnp.int32, (16, D), 1) // HEAD
        v.small[8:24, : 2 * 32] = lax.dot_general(
            (line == head).astype(F32),
            v.steps[...],
            (((1,), (1,)), ((), ())),
            precision=lax.Precision.HIGHEST,
            preferred_element_type=F32,
        )

    def run_first():
        start(*FIRST, *in_wq, "wo", *in_wu, *in_wd)
        wait(*FIRST)
        meta = grid_places(v.segment[...], cols)
        v.meta[0] = meta
        v.payload[ROWS:, :] = jnp.zeros((8, D), F32)
        v.payload[ROWS:, :ROWS] = meta
        for k in range(8):
            v.vecs[k : k + 1, :] = getattr(v, f"vector{k}")[...]
        for k in range(FF // D):
            v.vecs[8 + k : 9 + k, :] = v.up_bias[:, k * D : (k + 1) * D]
        v.tabs[...] = jnp.zeros((HEADS, 2 * SEQ), F32)
        for t in range(2):
            for head in range(HEADS):
                row, lane = t * 6 + head // 2, head % 2 * SEQ
                v.tabs[row : row + 1, lane : lane + NR] = v.rel[head, t : t + 1, :]

        @pl.when(section == 0)
        def _():
            for span in blocks():
                value = v.patches[span, :].astype(F32)
                v.x[span, :] = value
                v.payload[span, :] = value
            start("out_payload", "out_vecs", "out_tabs")
            forward([])
            wait(*in_wd)
            finish_layer()
            start("out_y", "out_output")
            wait("out_y", "out_output")

        @pl.when(section == 1)
        def _():
            for span in blocks():
                v.payload[span, :] = v.cotangent[span, :].astype(F32)
            start("out_payload", "out_vecs", "out_tabs")
            wait(*in_wq, "wo", *in_wu, *in_wd)

        wait("out_payload", "out_vecs", "out_tabs")

    def run_save():
        start("vecs", "tabs", *in_x, *in_meta, *in_wq, "wo", *in_wu)
        forward(in_x)
        wait(*stores)

    def run_own():
        start("vecs", "tabs", "b0", "meta0", *in_wq, "wo", *in_wu, "u_a0", *in_wd)
        forward(["b0"])
        wait("u_a0")
        backward_hidden()
        backward_middle()
        backward_attention()
        own_input_grad()
        store("out_grad")
        wait(*stores)

    def run_chunk():
        u_a, u_b = ([f"u_{side}{k}" for k in range(shards)] for side in "ab")
        in_b = [f"b{k}" for k in range(shards)]
        early = ["vecs", *u_b, "in_slope"]
        middle = [*in_wu, "in_normal2", "in_inverse2", "in_branch", "in_sel", "in_act_sel"]
        late = ["wo", "in_qkv", "in_probs"]
        own = ["a0", "meta0", "in_y", "in_output", *in_wq] if extras else []

        if saved:

            @pl.when(section == 0)
            def _():
                start(*early, *in_wd, *middle, *in_sums, *late, *own)
                wait(*early, *in_wd)

            @pl.when(section == 1)
            def _():
                start("vecs", "tabs", *in_b, *in_meta, *in_wq, "wo", *in_wu)
                start(*u_a, *in_wd, *in_sums)
                forward(in_b)
                wait(*u_a, *in_wd)
                if extras:
                    finish_layer()

        else:

            @pl.when(section == 0)
            def _():
                start(*in_x, *u_b)

            @pl.when(section == 1)
            def _():
                start(*in_b, *u_a)

            start("vecs", "tabs", *in_meta, *in_wq, "wo", *in_wu, *in_wd, *in_sums)
            forward(in_b)
            wait(*u_a)

        total_out = backward_hidden()

        if saved:
            pl.when(section == 0)(lambda: wait(*middle))

        wait(*in_sums)

        def add(name, where, value):
            ref = getattr(v, name)
            ref[where] = value if first else ref[where] + value

        everything = (slice(None), slice(None))
        add("sum_u", everything, dot(v.sel[2], v.dhid[...]))
        add("sum_d", everything, dot_lt(v.act_sel[...], v.dob[...]))
        if last:
            pack_rows(0)
        else:
            store("out_sum_u", "out_sum_d")
        totals = [total_out] + backward_middle()
        for k, total in enumerate(totals):
            add("sum_v", (slice(k, k + 1), slice(None)), column_sum(total))
        add("sum_o", everything, dot(v.sel[1], v.dbr[...]))
        if last:
            pack_rows(1)
        else:
            store("out_sum_o", "out_sum_v")

        if saved:
            pl.when(section == 0)(lambda: wait(*late))

        backward_attention()
        add("sum_q", everything, dot(v.sel[0], v.dqkv[...]))
        if last:
            pack_rows(2)
        else:
            store("out_sum_q")
        if extras:

            pl.when(section == 0)(lambda: wait(*own))
            store("out_y")
            own_extras()
            store("out_grad", "out_small")
        wait(*stores)

    def pack_rows(stage):
        core = lax.axis_index("dp") % 2
        half, quarter = SEL // 2, SELF // 8
        for side, target in enumerate(packs):
            whose = core if side == 0 else 1 - core
            low = pl.ds(pl.multiple_of(whose * half, 8), half)
            pieces = {}
            if stage == 0:
                pieces["u"] = (v.sum_u.at[low, :], target.at[:half, : 4 * D])
                for k in range(4):
                    start_row = pl.multiple_of(whose * (SELF // 2) + k * quarter, 8)
                    span = slice((8 + k) * D, (9 + k) * D)
                    piece = v.sum_d.at[pl.ds(start_row, quarter), :]
                    pieces[f"d{k}"] = (piece, target.at[:half, span])
            elif stage == 1:
                pieces["o"] = (v.sum_o.at[low, :], target.at[:half, 7 * D : 8 * D])
                tails = [v.sum_v.at[...], v.sum_o.at[SEL : SEL + 8, :]]
                tails += [v.sum_u.at[SEL : SEL + 8, k * D : (k + 1) * D] for k in range(FF // D)]
                for k, piece in enumerate(tails):
                    pieces[f"t{k}"] = (piece, target.at[half:, k * D : (k + 1) * D])
            else:
                pieces["q"] = (v.sum_q.at[low, :], target.at[:half, 4 * D : 7 * D])
            for name, piece in pieces.items():
                table[f"pack{side}{name}"] = piece
                store(f"pack{side}{name}")

    if kind == "fwd":
        run_first()
    elif kind == "save":
        pl.when(section == 0)(run_save)
    elif kind == "own":
        pl.when(section == 1)(run_own)
    else:
        run_chunk()


def run_layer(
    kind, vecs, tabs, weights, a_shards, b_shards=(), saved=(), output=None, sums=None, last=False
):
    shards = len(a_shards) if kind != "fwd" else 1
    hbm = pl.BlockSpec(memory_space=pl.ANY)
    smem = pl.BlockSpec(memory_space=pltpu.SMEM)
    extras, first = output is not None, sums is None
    ins = [vecs, tabs, *weights, *a_shards, *b_shards, *saved]
    if kind == "fwd":
        ins = [*a_shards, *weights]
    aliases = {}
    row_shape = jax.ShapeDtypeStruct((ROWS, D), F32)
    if kind == "fwd":
        outs = [
            jax.ShapeDtypeStruct((ROWS + 8, D), F32),
            jax.ShapeDtypeStruct((8 + FF // D, D), F32),
            jax.ShapeDtypeStruct((HEADS, 2 * SEQ), F32),
            row_shape,
            row_shape,
        ]
    elif kind == "own":
        outs = [row_shape]
    elif kind == "save":
        outs = saved_shapes(shards)
    else:
        if last:
            outs = [jax.ShapeDtypeStruct(PACK, F32)] * 2
        else:
            outs = [jax.ShapeDtypeStruct(shape, F32) for shape in SUM_SHAPES]
        if extras:
            ins += output
            outs += [jax.ShapeDtypeStruct((1, ROWS, D), F32)] * 2
            outs.append(jax.ShapeDtypeStruct((24, D), F32))
        if not first:
            if not last:
                aliases = {len(ins) + k: k for k in range(5)}
            ins += list(sums)
    return pl.pallas_call(
        functools.partial(layer_kernel, kind, shards, bool(saved), extras, first, last),
        out_shape=tuple(outs),
        in_specs=[smem if kind == "fwd" else hbm] + [hbm] * (len(ins) - 1),
        out_specs=(hbm,) * len(outs),
        scratch_shapes=[*Scratch(kind, shards).shapes, pltpu.SemaphoreType.DMA((96,))],
        input_output_aliases=aliases,
        compiler_params=pltpu.CompilerParams(vmem_limit_bytes=60 * 1024 * 1024),
        cost_estimate=pl.CostEstimate(
            flops=WORK[kind] * shards * ROWS, bytes_accessed=1000, transcendentals=0
        ),
        name="layer_" + kind,
    )(*ins)


def finish_kernel(kept, received, small_a, small_b, small_c, small_d, *outs):
    outs, (mine, other, sems) = outs[:-3], outs[-3:]
    grad_q, grad_o, grad_u, grad_d, grad_ub, grad_table, *vectors = outs
    half = SEL // 2
    spans = [slice(0, 4 * D), slice(4 * D, 8 * D), slice(8 * D, 12 * D)]
    copies = []
    for k, span in enumerate(spans):
        copies.append(
            [
                pltpu.make_async_copy(kept.at[:, span], mine.at[:, span], sems.at[2 * k]),
                pltpu.make_async_copy(received.at[:, span], other.at[:, span], sems.at[2 * k + 1]),
            ]
        )
        for one in copies[-1]:
            one.start()
    device = lax.axis_index("dp")

    def total(lines, lanes):
        return mine[lines, lanes] + other[lines, lanes]

    body_rows, tail_rows = slice(0, half), slice(half, half + 8)
    for one in copies[0]:
        one.wait()
    grad_u[0] = total(body_rows, spans[0])
    for one in copies[1]:
        one.wait()
    sums_low, sums_out = (total(tail_rows, slice(k * D, (k + 1) * D)) for k in range(2))
    sums_up = [total(tail_rows, slice((2 + k) * D, (3 + k) * D))[:1] for k in range(FF // D)]
    small_all = (small_a[...] + small_b[...]) + (small_c[...] + small_d[...])
    small = [small_all[:8], small_all[8:16]]
    width = vectors[0].shape[1]
    sources = (
        (small[0], 1),
        (small[0], 2),
        (sums_out, 0),
        (sums_low, 3),
        (sums_low, 1),
        (sums_low, 2),
        (sums_low, 0),
        (small[0], 0),
    )
    for out, (source, line) in zip(vectors, sources):
        out[...] = pltpu.roll(source, D - device * width, 1)[line : line + 1, :width]
    wide = grad_ub.shape[1]
    first = device * wide
    row = sums_up[0]
    for k in range(1, FF // D):
        row = jnp.where(first // D == k, sums_up[k], row)
    turned = pltpu.roll(jnp.broadcast_to(row, (8, D)), D - first % D, 1)
    grad_ub[...] = turned[:1, :wide]
    grad_q[0] = total(body_rows, slice(4 * D, 7 * D))
    grad_o[0] = total(body_rows, slice(7 * D, 8 * D))
    for one in copies[2]:
        one.wait()
    heads_low, heads_high = small[1], small_all[16:]
    for t in range(2):
        span = slice(32 * t, 32 * t + NR)
        for head in range(HEADS):
            held = heads_low if head < 8 else heads_high
            grad_table[0, head, t : t + 1, :] = held[head % 8 : head % 8 + 1, span]
    for k in range(4):
        grad_d[0, k * half : (k + 1) * half, :] = total(
            body_rows, slice((8 + k) * D, (9 + k) * D)
        )


def body(
    patches,
    cotangent,
    seg_ids,
    grid_cols,
    norm_gain1,
    norm_bias1,
    qkv_weight,
    out_weight,
    out_bias,
    attn_scale,
    norm_gain2,
    norm_bias2,
    up_weight,
    up_bias,
    down_weight,
    down_bias,
    mlp_scale,
    rel_table,
):
    dp_count = lax.axis_size("dp")
    supers = dp_count // (2 * BLOCK)
    section = lax.axis_index("section")
    device = lax.axis_index("dp")
    core = device % 2
    def pairs(move):
        return [
            (2 * (b * supers + s) + c, 2 * (move(b) * supers + s) + c)
            for b in range(BLOCK)
            for s in range(supers)
            for c in range(2)
        ]

    def along(array, step):
        return lax.ppermute(array, "dp", pairs(lambda b: (b // 2 + step) % 4 * 2 + b % 2))

    def across(array):
        return lax.ppermute(array, "dp", pairs(lambda b: b ^ 1))

    def diagonal(array):
        moves = [(source, target ^ 1) for source, target in pairs(lambda b: b ^ 1)]
        return lax.ppermute(array, "dp", moves)

    def sibling(array):
        return lax.ppermute(array, "dp", [(d, d ^ 1) for d in range(dp_count)])

    vectors = (
        norm_gain1,
        norm_bias1,
        out_bias,
        attn_scale,
        norm_gain2,
        norm_bias2,
        down_bias,
        mlp_scale,
        up_bias,
    )
    weights = (qkv_weight[0], out_weight[0], up_weight[0], down_weight[0])

    def after(array, *others):
        return lax.optimization_barrier((array, *others))[0]

    firsts = [
        grid_cols,
        seg_ids.reshape(1, ROWS),
        rel_table[0].transpose(1, 0, 2),
        patches,
        cotangent,
        *vectors,
    ]
    own, vecs, tabs, y0, output0 = run_layer("fwd", None, None, weights, firsts)

    def layer(kind, *rest, **named):
        return run_layer(kind, vecs, tabs, weights, *rest, **named)

    def flipped(array, flip):
        return lax.ppermute(array, "dp", pairs(lambda b: b ^ flip))

    x1 = lax.ppermute(y0, "section", [(0, 1)])
    a_y = across(own)
    a_z = [along(own, step) for step in (1, 3)]
    (grad1,) = layer("own", [own], [x1])
    u0 = lax.ppermute(grad1, "section", [(1, 0)])
    own_then = after(own, grad1)
    a_z.append(along(own_then, 2))
    kept = layer("save", [own_then, a_y])
    a_yz = [across(after(piece, kept[0])) for piece in a_z[:2]]
    b_own = jnp.where(section == 0, after(u0, kept[0], a_z[2]), x1)
    b_y = across(b_own)
    b_z = [along(b_own, step) for step in (1, 3)]
    b_z.append(along(after(b_own, b_y, *a_yz), 2))
    a_yz.append(across(after(a_z[2], b_y, *a_yz)))
    *sums, section_out, section_grad, small = layer(
        "chunk",
        [own, a_y],
        [b_own, b_y],
        (after(kept[0], *a_yz[:2]), *kept[1:]),
        (y0, output0),
    )
    b_z = [after(piece, small) for piece in b_z]
    b_yz = [across(piece) for piece in b_z]
    moved = flipped(small, 4)
    sums = layer("chunk", [after(a_z[0], a_yz[2]), *a_z[1:]], b_z, (), None, sums)
    small = small + after(moved, sums[0])
    moved = flipped(small, 2)
    last_a = [after(a_yz[0], small), *a_yz[1:]]
    sums = layer("chunk", last_a, b_yz, (), None, sums, supers == 1)
    small = small + after(moved, sums[0])
    width = D // dp_count
    wide = FF // dp_count
    if supers == 1:
        mine, others = sums
        hbm = pl.BlockSpec(memory_space=pl.ANY)
        shapes = [(1, width, 3 * D), (1, width, D), (1, width, FF), (1, wide, D), (1, wide)]
        shapes += [(1, HEADS, 2, NR)] + [(1, width)] * 8
        grad_q, grad_o, grad_u, grad_d, grad_ub, grad_table, *vectors = pl.pallas_call(
            finish_kernel,
            out_shape=tuple(jax.ShapeDtypeStruct(shape, F32) for shape in shapes),
            in_specs=[hbm, hbm] + [pl.BlockSpec()] * 4,
            scratch_shapes=[
                pltpu.VMEM(PACK, F32),
                pltpu.VMEM(PACK, F32),
                pltpu.SemaphoreType.DMA((6,)),
            ],
            compiler_params=pltpu.CompilerParams(vmem_limit_bytes=32 * 1024 * 1024),
            name="finish",
        )(mine, sibling(others), small, across(small), sibling(small), diagonal(small))
        grad_table = grad_table.transpose(0, 2, 1, 3)
    else:
        sum_u, sum_d, sum_o, sum_q, sum_v = sums
        sum_v = jnp.concatenate(
            [sum_v[:4], sum_o[SEL : SEL + 1], sum_u[SEL : SEL + 1].reshape(FF // D, D)], axis=0
        )

        def shifted(array, step):
            moves = [
                (2 * (b * supers + s) + c, 2 * (b * supers + (s + step) % supers) + c)
                for b in range(BLOCK)
                for s in range(supers)
                for c in range(2)
            ]
            return lax.ppermute(array, "dp", moves)

        def scatter(partial):
            parts = partial.reshape(supers, 2, partial.shape[0] // (2 * supers), partial.shape[1])
            held = lax.dynamic_index_in_dim(parts, core, 1, keepdims=False)
            held = held + sibling(lax.dynamic_index_in_dim(parts, 1 - core, 1, keepdims=False))
            place = device // 2 % supers
            total = lax.dynamic_index_in_dim(held, place, 0, keepdims=False)
            for step in range(1, supers):
                there = (place + step) % supers
                total = total + shifted(
                    lax.dynamic_index_in_dim(held, there, 0, keepdims=False), step
                )
            return total[None]

        small = small + across(small)
        sums = jnp.concatenate([sum_v, small[:8], small[8:]], axis=0)
        sums = sums + sibling(sums)
        sums = sums + sum(shifted(sums, step) for step in range(1, supers))
        vectors = [
            lax.dynamic_slice(sums, (row, device * width), (1, width))
            for row in (10, 11, 4, 3, 1, 2, 0, 9)
        ]
        grad_ub = lax.dynamic_slice(sums[5:9].reshape(1, FF), (0, device * wide), (1, wide))
        grad_table = sums[17 : 17 + HEADS, :64].reshape(HEADS, 2, 32)[:, :, :NR]
        grad_table = grad_table.transpose(1, 0, 2)[None]
        grad_q, grad_o, grad_u, grad_d = (
            scatter(partial) for partial in (sum_q[:SEL], sum_o[:SEL], sum_u[:SEL], sum_d)
        )
    gain1, bias1, out_b, attn, gain2, bias2, down_b, mlp = vectors
    return (
        section_out,
        section_grad,
        gain1,
        bias1,
        grad_q,
        grad_o,
        out_b,
        attn,
        gain2,
        bias2,
        grad_u,
        grad_ub,
        grad_d,
        down_b,
        mlp,
        grad_table,
    )


def solution(mesh):
    row, whole = P("dp", None), P("section", None)
    matrix = P("section", None, None)
    in_specs = (
        row,
        row,
        P("dp"),
        row,
        whole,
        whole,
        matrix,
        matrix,
        whole,
        whole,
        whole,
        whole,
        matrix,
        whole,
        matrix,
        whole,
        whole,
        P("section", None, None, None),
    )
    tokens, vector, weight = P("section", "dp", None), P("section", "dp"), P("section", "dp", None)
    out_specs = (
        tokens,
        tokens,
        vector,
        vector,
        weight,
        weight,
        vector,
        vector,
        vector,
        vector,
        weight,
        vector,
        weight,
        vector,
        vector,
        P("section", None, None, None),
    )
    return jax.shard_map(body, mesh=mesh, in_specs=in_specs, out_specs=out_specs, check_vma=False)
```

```python
import functools
import math

import jax
import jax.numpy as jnp
from jax import lax
from jax.experimental import pallas as pl
from jax.experimental.pallas import tpu as pltpu
from jax.sharding import PartitionSpec as P

D = 768
HEADS = 12
HEAD = 64
FF = 3072
RMAX = 15
NR = 31
SEQ = 64
ROWS = 128
BLOCK = 8
GROUP = 4 * HEAD
GROUPS = D // GROUP
TILE = 768
STEP = 32
BATCH = 6
AHEAD = 3
FINE = 256
TILES = FF // TILE
SEL = D // BLOCK
SELP = SEL + 16
SELF = FF // BLOCK

EPSILON = 1e-06
WORK = {"fwd": 1, "own": 1, "save": 1, "chunk": 1}
MASKED = -1e30
C0 = math.sqrt(2.0 / math.pi)
C1 = C0 * 0.044715
F32 = jnp.float32
BF16 = jnp.bfloat16


def dot(left, right):
    return lax.dot_general(left, right, (((1,), (0,)), ((), ())), preferred_element_type=F32)


def dot_rt(left, right):
    return lax.dot_general(left, right, (((1,), (1,)), ((), ())), preferred_element_type=F32)


def dot_lt(left, right):
    return lax.dot_general(left, right, (((0,), (0,)), ((), ())), preferred_element_type=F32)


def normalize(rows):
    shifted = rows - jnp.mean(rows, axis=-1, keepdims=True)
    inverse = lax.rsqrt(jnp.mean(shifted * shifted, axis=-1, keepdims=True) + EPSILON)
    return shifted * inverse, inverse


def normalize_back(grad, normal, inverse):
    mean_grad = jnp.mean(grad, axis=-1, keepdims=True)
    mean_both = jnp.mean(grad * normal, axis=-1, keepdims=True)
    return (grad - mean_grad - normal * mean_both) * inverse


def column_sum(rows):
    return jnp.sum(rows, axis=0, keepdims=True)


def grid_places(segment, cols):
    lane = lax.broadcasted_iota(jnp.int32, (1, ROWS), 1)
    place = (lane % SEQ).astype(F32)
    second = lane >= SEQ
    start = jnp.zeros((1, ROWS), F32)
    width = jnp.zeros((1, ROWS), F32)
    before_first = jnp.zeros((1, 1), F32)
    before_second = jnp.zeros((1, 1), F32)
    for page in range(cols.shape[1]):
        member = segment == page
        ones = member.astype(F32)
        start += jnp.where(member, jnp.where(second, before_second, before_first), 0.0)
        width += jnp.where(member, jnp.where(second, cols[1, page], cols[0, page]).astype(F32), 0.0)
        before_first += jnp.sum(jnp.where(second, 0.0, ones), axis=1, keepdims=True)
        before_second += jnp.sum(jnp.where(second, ones, 0.0), axis=1, keepdims=True)
    offset = place - start
    width = jnp.maximum(width, 1.0)
    grid_row = jnp.floor((offset + 0.5) / width)
    grid_col = offset - grid_row * width
    line = lax.broadcasted_iota(jnp.int32, (8, ROWS), 0)
    return jnp.where(
        line == 0, segment.astype(F32), jnp.where(line == 1, grid_row, grid_col)
    )


def steps_of(meta, part):
    shape = (SEQ, ROWS)
    lane = lax.broadcasted_iota(jnp.int32, shape, 1)
    line = lax.broadcasted_iota(jnp.int32, shape, 0)
    left = lane < SEQ

    def across(values):
        wide = jnp.broadcast_to(values, (8, ROWS))
        swapped = pltpu.roll(wide, SEQ, 1)
        low = lax.broadcasted_iota(jnp.int32, (8, ROWS), 1) < SEQ
        both = jnp.where(low, wide, swapped) if part == 0 else jnp.where(low, swapped, wide)
        return both[:1]

    def down(values):
        return jnp.broadcast_to(values, (ROWS, ROWS)).T[part * SEQ : (part + 1) * SEQ, :]

    seg_i, row_i, col_i = (across(meta[k : k + 1]) for k in range(3))
    seg_j, row_j, col_j = (down(meta[k : k + 1]) for k in range(3))
    allowed = ((seg_i == seg_j) & (seg_j >= 0.0)) | ((lane % SEQ) == line)
    base = jnp.where(left, RMAX, RMAX + SEQ)
    row_step = jnp.clip(row_i - row_j, -RMAX, RMAX).astype(jnp.int32) + base
    col_step = jnp.clip(col_i - col_j, -RMAX, RMAX).astype(jnp.int32) + base
    return row_step, col_step, allowed


def fill_bias(meta, tabs, bias, first, part):
    if True:
        row_step, col_step, allowed = steps_of(meta, part)
        for pair in range(HEADS // 2):
            by_row = jnp.broadcast_to(tabs[pair : pair + 1, :], (SEQ, ROWS))
            by_col = jnp.broadcast_to(tabs[6 + pair : 7 + pair, :], (SEQ, ROWS))
            both = jnp.take_along_axis(by_row, row_step, axis=1) + jnp.take_along_axis(
                by_col, col_step, axis=1
            )
            bias[first + part, :, pair * ROWS : (pair + 1) * ROWS] = jnp.where(allowed, both, MASKED)


def diagonal_mask():
    line = lax.broadcasted_iota(jnp.int32, (GROUP, GROUP), 0) // HEAD
    lane = lax.broadcasted_iota(jnp.int32, (GROUP, GROUP), 1) // HEAD
    return line == lane


def spread(block, mask):
    return jnp.where(mask, jnp.concatenate([block] * 4, axis=0), jnp.zeros((), block.dtype))


def gather_diagonal(full):
    lane = lax.broadcasted_iota(jnp.int32, (SEQ, GROUP), 1) // HEAD
    result = full[:SEQ]
    for head in range(1, 4):
        result = jnp.where(lane == head, full[head * SEQ : (head + 1) * SEQ], result)
    return result


class Row:
    def __init__(self, ref, k):
        self.ref, self.k = ref, k

    def __call__(self):
        return self.ref[self.k : self.k + 1, :]


SUM_NAMES = ("sum_u", "sum_d", "sum_o", "sum_q", "sum_v")
SUM_SHAPES = ((SELP, FF), (SELF, D), (SELP, D), (SELP, 3 * D), (8, D))
FIRST = ("segment", "rel", "patches", "cotangent", *(f"vector{k}" for k in range(8)), "up_bias")
SAVED = ("slope", "normal2", "inverse2", "branch", "sel", "act_sel", "qkv", "probs")
SHARED = {"a": "x", "b": "x", "u_a": "u", "u_b": "u"}
PACK = (SEL // 2 + 8, 4 * D + 3 * D + D + 4 * D)


class Scratch:
    def __init__(self, kind, shards):
        rows, seqs = shards * ROWS, 2 * shards
        spec = {
            "vecs": ((8 + FF // D, D), F32),
            "tabs": ((HEADS, 2 * SEQ), F32),
            "wq": ((D, 3 * D), BF16),
            "wo": ((D, D), BF16),
            "wu": ((D, FF), BF16),
            "x": ((rows, D), F32),
            "meta": ((shards, 8, ROWS), F32),
            "normed": ((rows, D), BF16),
            "qkv": ((rows, 3 * D), BF16),
            "bias": ((seqs, SEQ, D), F32),
            "probs": ((seqs, SEQ, D), BF16),
            "mixed": ((rows, D), BF16),
            "branch": ((rows, D), F32),
            "normal2": ((rows, D), F32),
            "inverse2": ((rows, ROWS), F32),
            "n2b": ((rows, D), BF16),
            "act": ((rows, FF), BF16),
            "slope": ((rows, FF), BF16),
        }
        if kind != "save":
            spec["wd"] = ((FF, D), BF16)
        if kind in ("save", "chunk"):
            spec["act_sel"] = ((rows, SELF), BF16)
            spec["sel"] = ((3, SELP, rows), BF16)
        if kind == "fwd":
            spec.update((f"vector{k}", ((1, D), F32)) for k in range(8))
            spec["up_bias"] = ((1, FF), F32)
            spec["segment"] = ((1, ROWS), jnp.int32)
            spec["rel"] = ((HEADS, 2, NR), F32)
            spec["patches"] = ((ROWS, D), BF16)
            spec["cotangent"] = ((ROWS, D), BF16)
            spec["payload"] = ((ROWS + 8, D), F32)
        if kind in ("fwd", "chunk"):
            spec["middle"] = ((ROWS, D), F32)
            spec["y"] = ((ROWS, D), F32)
            spec["output"] = ((ROWS, D), F32)
        if kind in ("own", "chunk"):
            spec.update(
                u=((rows, D), F32),
                dob=((rows, D), BF16),
                dn2=((rows, D), F32),
                dbr=((rows, D), BF16),
                dmix=((rows, D), BF16),
                dqkv=((rows, 3 * D), BF16),
                dhid=((rows, FF), BF16),
                grad=((ROWS, D), F32),
            )
        if kind == "chunk":
            spec.update(zip(SUM_NAMES, ((shape, F32) for shape in SUM_SHAPES)))
            spec["small"] = ((24, D), F32)
            spec["steps"] = ((64, D), F32)
            spec["ds"] = ((2, SEQ, D), BF16)
        self.names = list(spec)
        self.shapes = [pltpu.VMEM(*spec[name]) for name in spec]

    def bind(self, refs):
        for name, ref in zip(self.names, refs):
            setattr(self, name, ref)
        return self


def saved_shapes(shards):
    scratch = Scratch("save", shards)
    shapes = dict(zip(scratch.names, scratch.shapes))
    return [jax.ShapeDtypeStruct(shapes[name].shape, shapes[name].dtype) for name in SAVED]


def layer_kernel(kind, shards, split, extras, first, last, *refs):
    refs = list(refs)

    def take(count):
        taken = refs[:count]
        del refs[:count]
        return taken

    rows = shards * ROWS
    seqs = 2 * shards
    if kind == "fwd":
        cols, *first_ins = take(1 + len(FIRST))
    else:
        vecs, tabs = take(2)
    wq, wo, wu, wd = take(4)
    a_refs = take(shards) if kind != "fwd" else []
    b_refs = take(shards) if kind in ("own", "chunk") else []
    saved = take(len(SAVED)) if kind == "chunk" and split else []
    y_in, output_in = take(2) if extras else (None, None)
    sums_in = take(5) if kind == "chunk" and not first else []
    outs = {}
    if kind == "fwd":
        outs = dict(zip(("payload", "vecs", "tabs", "y", "output"), take(5)))
    elif kind == "own":
        outs = dict(zip(("grad",), take(1)))
    elif kind == "save":
        outs = dict(zip(SAVED, take(len(SAVED))))
    elif last:
        packs = take(2)
    else:
        outs = dict(zip(SUM_NAMES, take(5)))
    if extras:
        outs.update(zip(("y", "grad", "small"), take(3)))
    scratch = Scratch(kind, shards)
    v = scratch.bind(take(len(scratch.names)))
    (sems,) = take(1)
    section = lax.axis_index("section")
    gain1, bias1, out_bias, attn_scale, gain2, bias2, down_bias, mlp_scale = (
        Row(v.vecs, k) for k in range(8)
    )
    index = {}
    tiles = [slice(k * TILE, (k + 1) * TILE) for k in range(TILES)]
    thirds = [slice(k * D, (k + 1) * D) for k in range(3)]
    shard_rows = [slice(k * ROWS, (k + 1) * ROWS) for k in range(shards)]
    table = {"wo": (wo, v.wo)}
    if kind == "fwd":
        table.update((name, (ref, getattr(v, name))) for name, ref in zip(FIRST, first_ins))
    else:
        table.update(vecs=(vecs, v.vecs), tabs=(tabs, v.tabs))
    for k, span in enumerate(thirds):
        table[f"wq{k}"] = (wq.at[:, span], v.wq.at[:, span])
    for k, span in enumerate(tiles):
        table[f"wu{k}"] = (wu.at[:, span], v.wu.at[:, span])
        if kind != "save":
            table[f"wd{k}"] = (wd.at[span, :], v.wd.at[span, :])
    for k, span in enumerate(shard_rows if a_refs else []):
        table[f"a{k}"] = (a_refs[k].at[:ROWS, :], v.x.at[span, :])
        table[f"meta{k}"] = (a_refs[k].at[ROWS : ROWS + 8, :ROWS], v.meta.at[k])
        if kind in ("own", "chunk"):
            table[f"u_a{k}"] = (a_refs[k].at[:ROWS, :], v.u.at[span, :])
            table[f"u_b{k}"] = (b_refs[k], v.u.at[span, :])
            table[f"b{k}"] = (b_refs[k], v.x.at[span, :])
    for k, ref in enumerate(saved):
        table["in_" + SAVED[k]] = (ref, getattr(v, SAVED[k]))
    for k, ref in enumerate(sums_in):
        table["in_" + SUM_NAMES[k]] = (ref, getattr(v, SUM_NAMES[k]))
    if extras:
        table["in_y"] = (y_in, v.y)
        table["in_output"] = (output_in, v.output)
    for name, ref in outs.items():
        if name == "slope" or name == "qkv":
            for k, span in enumerate(tiles if name == "slope" else thirds):
                table[f"out_{name}{k}"] = (getattr(v, name).at[:, span], ref.at[:, span])
        else:
            target = ref.at[0] if extras and name in ("y", "grad") else ref
            table["out_" + name] = (getattr(v, name), target)
    in_x = [f"a{k}" for k in range(shards)]
    in_meta = [f"meta{k}" for k in range(shards)]
    in_wq = ["wq0", "wq1", "wq2"]
    in_wu = [f"wu{k}" for k in range(TILES)]
    in_wd = [f"wd{k}" for k in range(TILES)]
    in_sums = ["in_" + name for name in SUM_NAMES] if sums_in else []
    stores = []

    def descriptor(name):
        source, target = table[name]
        shared = SHARED.get(name[:-1], name[:-1]) + name[-1]
        return pltpu.make_async_copy(source, target, sems.at[index.setdefault(shared, len(index))])

    def start(*names):
        for name in names:
            descriptor(name).start()

    def wait(*names):
        for name in names:
            descriptor(name).wait()

    def store(*names):
        start(*names)
        stores.extend(names)

    def blocks(count=shards):
        for first_row in range(0, count * ROWS, STEP):
            yield slice(first_row, first_row + STEP)

    def fold(total, values):
        for first_row in range(0, STEP, 8):
            total = total + values[first_row : first_row + 8]
        return total

    def pipelined(items, *stages):
        held = {}
        for k in range(len(items) + len(stages) - 1):
            for depth, stage in enumerate(stages):
                if 0 <= k - depth < len(items):
                    item = items[k - depth]
                    held[k - depth] = stage(item, held.get(k - depth))

    def centre(values):
        return values - jnp.mean(values, axis=-1, keepdims=True)

    def inverse_of(shifted):
        return lax.rsqrt(jnp.mean(shifted * shifted, axis=-1, keepdims=True) + EPSILON)

    def forward(x_names):
        if kind != "fwd":
            wait("vecs", "tabs", *x_names, *in_meta)
        def norm_store(span, held):
            shifted, inverse = held
            v.normed[span, :] = (shifted * inverse * gain1() + bias1()).astype(BF16)

        pipelined(
            list(blocks()),
            lambda span, _: centre(v.x[span, :]),
            lambda span, shifted: (shifted, inverse_of(shifted)),
            norm_store,
        )
        wait(*in_wq)
        fill = [(shard, half) for shard in range(shards) for half in range(2)]
        for k, cols in enumerate(thirds):
            v.qkv[:, cols] = dot(v.normed[...], v.wq[:, cols]).astype(BF16)
            for shard, half in fill[k * len(fill) // 3 : (k + 1) * len(fill) // 3]:
                fill_bias(v.meta[shard], v.tabs, v.bias, 2 * shard, half)
        if kind == "save":
            store(*(f"out_qkv{k}" for k in range(3)))
        mask = diagonal_mask()
        units = [(s, g) for s in range(seqs) for g in range(GROUPS)]

        def score(unit):
            s, g = unit
            span, cols = slice(s * SEQ, (s + 1) * SEQ), slice(g * GROUP, (g + 1) * GROUP)
            query = v.qkv[span, cols] * BF16(0.125)
            key = v.qkv[span, D + g * GROUP : D + (g + 1) * GROUP]
            return dot_rt(key, spread(query, mask)) + v.bias[s, :, cols]

        def soften(unit, scores):
            s, g = unit
            grown = jnp.exp(scores - jnp.max(scores, axis=0, keepdims=True))
            prob = (grown * (1.0 / jnp.sum(grown, axis=0, keepdims=True))).astype(BF16)
            if kind != "fwd":
                v.probs[s, :, g * GROUP : (g + 1) * GROUP] = prob
            return prob

        def mix(unit, prob):
            s, g = unit
            span, cols = slice(s * SEQ, (s + 1) * SEQ), slice(g * GROUP, (g + 1) * GROUP)
            value = v.qkv[span, 2 * D + g * GROUP : 2 * D + (g + 1) * GROUP]
            v.mixed[span, cols] = gather_diagonal(dot_lt(prob, value)).astype(BF16)

        batches = [units[k : k + AHEAD] for k in range(0, len(units), AHEAD)]
        waiting_scores, waiting_probs = {}, {}
        for k in range(len(batches) + 2):
            if k < len(batches):
                waiting_scores[k] = [score(unit) for unit in batches[k]]
            if 0 <= k - 1 < len(batches):
                pairs = zip(batches[k - 1], waiting_scores.pop(k - 1))
                waiting_probs[k - 1] = [soften(unit, scores) for unit, scores in pairs]
            if 0 <= k - 2 < len(batches):
                for unit, prob in zip(batches[k - 2], waiting_probs.pop(k - 2)):
                    mix(unit, prob)

        if kind == "save":
            store("out_probs")
        wait("wo")
        v.branch[...] = dot(v.mixed[...], v.wo[...])
        def middle_of(span, _):
            branch_value = v.branch[span, :] + out_bias()
            v.branch[span, :] = branch_value
            middle_value = v.x[span, :] + attn_scale() * branch_value
            if (kind == "fwd" or extras) and span.start < ROWS:
                v.middle[span, :] = middle_value
            return centre(middle_value)

        def norm2_store(span, held):
            shifted, inverse = held
            normal2 = shifted * inverse
            if kind != "fwd":
                v.normal2[span, :] = normal2
                v.inverse2[span, :] = jnp.broadcast_to(inverse, (STEP, ROWS))
            v.n2b[span, :] = (normal2 * gain2() + bias2()).astype(BF16)

        pipelined(
            list(blocks()),
            middle_of,
            lambda span, shifted: (shifted, inverse_of(shifted)),
            norm2_store,
        )
        if kind == "save":
            store("out_normal2", "out_inverse2", "out_branch")
        wait(*in_wu)

        def hidden_of(low):
            return dot(v.n2b[...], v.wu[:, low : low + FINE])

        def activate(low, hidden):
            row, lane = 8 + low // D, low % D
            hidden = (hidden + v.vecs[row : row + 1, lane : lane + FINE]).astype(BF16)
            square = hidden * hidden
            share = 0.5 + 0.5 * jnp.tanh(hidden * (C0 + C1 * square))
            active = hidden * share
            v.act[:, low : low + FINE] = active.astype(BF16)
            if kind != "fwd":
                slope = share + active * (1.0 - share) * (2.0 * C0 + 6.0 * C1 * square)
                v.slope[:, low : low + FINE] = slope.astype(BF16)

        held = hidden_of(0)
        for low in range(0, FF, FINE):
            ahead = hidden_of(low + FINE) if low + FINE < FF else None
            activate(low, held)
            held = ahead
        if kind == "save":
            store(*(f"out_slope{k}" for k in range(TILES)))
        if kind in ("save", "chunk"):
            place = lax.axis_index("dp") // (lax.axis_size("dp") // BLOCK)
            line = lax.broadcasted_iota(jnp.int32, (SEL, D), 0)
            lane = lax.broadcasted_iota(jnp.int32, (SEL, D), 1)
            pick = (lane == line + place * SEL).astype(BF16)
            for k, source in enumerate((v.normed, v.mixed, v.n2b)):
                v.sel[k, :SEL] = dot_rt(pick, source[...]).astype(BF16)
                v.sel[k, SEL:] = jnp.ones((SELP - SEL, rows), BF16)
            v.act_sel[...] = v.act[:, pl.ds(pl.multiple_of(place * SELF, ROWS), SELF)]
        if kind == "save":
            store("out_sel", "out_act_sel")

    def backward_hidden():
        total_out = jnp.zeros((8, D), F32)
        for span in blocks():
            d_output = (mlp_scale() * v.u[span, :]).astype(BF16)
            v.dob[span, :] = d_output
            total_out = fold(total_out, d_output.astype(F32))
        if not split:
            wait(*in_wd)

        def slide(low, d_act):
            fine = slice(low, low + FINE)
            v.dhid[:, fine] = d_act.astype(BF16) * v.slope[:, fine]

        pipelined(
            list(range(0, FF, FINE)),
            lambda low, _: dot_rt(v.dob[...], v.wd[low : low + FINE, :]),
            slide,
        )
        return total_out

    def backward_middle():
        v.dn2[...] = dot_rt(v.dhid[...], v.wu[...])
        totals = [jnp.zeros((8, D), F32)] * 3

        def means(span, _):
            normal2 = v.normal2[span, :]
            grad = v.dn2[span, :] * gain2()
            mean_grad = jnp.mean(grad, axis=-1, keepdims=True)
            return mean_grad, jnp.mean(grad * normal2, axis=-1, keepdims=True)

        def finish(span, held):
            mean_grad, mean_both = held
            normal2, d_n2 = v.normal2[span, :], v.dn2[span, :]
            inverse2 = v.inverse2[span, :1]
            back = (d_n2 * gain2() - mean_grad - normal2 * mean_both) * inverse2
            d_middle = v.u[span, :] + back
            v.dbr[span, :] = (attn_scale() * d_middle).astype(BF16)
            if (kind == "own" or extras) and span.start < ROWS:
                v.grad[span, :] = d_middle
            if kind == "chunk":
                terms = (d_n2 * normal2, d_n2, d_middle * v.branch[span, :])
                totals[:] = [fold(total, term) for total, term in zip(totals, terms)]

        pipelined(list(blocks()), means, finish)
        return totals

    def backward_attention():
        v.dmix[...] = dot_rt(v.dbr[...], v.wo[...]).astype(BF16)
        mask = diagonal_mask()
        units = [(s, g) for s in range(seqs) for g in range(GROUPS)]
        batches = [units[k : k + BATCH] for k in range(0, len(units), BATCH)]

        def where_of(unit):
            s, g = unit
            return slice(s * SEQ, (s + 1) * SEQ), [
                slice(k * D + g * GROUP, k * D + (g + 1) * GROUP) for k in range(3)
            ]

        def probs_back(batch, _):
            made = []
            for unit in batch:
                span, cols = where_of(unit)
                d_mix = spread(v.dmix[span, cols[0]], mask)
                made.append((dot_rt(v.qkv[span, cols[2]], d_mix), d_mix))
            return made

        def scores_back(batch, held):
            made = []
            for unit, (d_prob, d_mix) in zip(batch, held):
                _, cols = where_of(unit)
                prob = v.probs[unit[0], :, cols[0]]
                wide = prob.astype(F32)
                delta = jnp.sum(wide * d_prob, axis=0, keepdims=True)
                d_score = (wide * (d_prob - delta)).astype(BF16)
                if extras and unit[0] < 2:
                    v.ds[unit[0], :, cols[0]] = d_score
                made.append((d_score, prob, d_mix))
            return made

        def inputs_back(batch, held):
            for unit, (d_score, prob, d_mix) in zip(batch, held):
                span, cols = where_of(unit)
                query = spread(v.qkv[span, cols[0]] * BF16(0.125), mask)
                d_query = gather_diagonal(dot_lt(d_score, v.qkv[span, cols[1]])) * 0.125
                v.dqkv[span, cols[0]] = d_query.astype(BF16)
                v.dqkv[span, cols[1]] = dot(d_score, query).astype(BF16)
                v.dqkv[span, cols[2]] = dot(prob, d_mix).astype(BF16)

        pipelined(batches, probs_back, scores_back, inputs_back)

    def own_input_grad():
        v.dn2[:ROWS, :] = dot_rt(v.dqkv[:ROWS, :], v.wq[...])
        totals = [jnp.zeros((8, D), F32)] * 3

        def finish(span, held):
            shifted, inverse = held
            d_normed, normal = v.dn2[span, :], shifted * inverse
            if extras:
                terms = (v.u[span, :] * v.output[span, :], d_normed * normal, d_normed)
                totals[:] = [fold(total, term) for total, term in zip(totals, terms)]
            v.grad[span, :] += normalize_back(d_normed * gain1(), normal, inverse)

        pipelined(
            list(blocks(1)),
            lambda span, _: centre(v.x[span, :]),
            lambda span, shifted: (shifted, inverse_of(shifted)),
            finish,
        )
        return totals

    def finish_layer():
        output = dot(v.act[:ROWS, :], v.wd[...]) + down_bias()
        v.output[...] = output
        v.y[...] = v.middle[...] + mlp_scale() * output

    def own_extras():
        totals = own_input_grad()
        v.small[...] = jnp.zeros((24, D), F32)
        for k in range(3):
            v.small[k : k + 1, :] = column_sum(totals[k])
        v.steps[...] = jnp.zeros((64, D), F32)
        lane = lax.broadcasted_iota(jnp.int32, (SEQ, ROWS), 1)
        steps = [steps_of(v.meta[0], half) for half in range(2)]
        for pair in range(HEADS // 2):
            span = slice(pair * ROWS, (pair + 1) * ROWS)
            grads = [v.ds[half, :, span].astype(F32) for half in range(2)]
            for which, low, high in ((0, 0, NR), (1, RMAX - 7, RMAX + 8)):
                for r in range(low, high):
                    total = jnp.zeros((8, ROWS), F32)
                    for half in range(2):
                        step = steps[half][which] - jnp.where(lane < SEQ, 0, SEQ)
                        chosen = jnp.where(step == r, grads[half], 0.0)
                        for line in range(0, SEQ, 8):
                            total = total + chosen[line : line + 8]
                    v.steps[32 * which + r : 32 * which + r + 1, span] = column_sum(total)
        line = lax.broadcasted_iota(jnp.int32, (16, D), 0)
        head = lax.broadcasted_iota(jnp.int32, (16, D), 1) // HEAD
        v.small[8:24, : 2 * 32] = lax.dot_general(
            (line == head).astype(F32),
            v.steps[...],
            (((1,), (1,)), ((), ())),
            precision=lax.Precision.HIGHEST,
            preferred_element_type=F32,
        )

    def run_first():
        start(*FIRST, *in_wq, "wo", *in_wu, *in_wd)
        wait(*FIRST)
        meta = grid_places(v.segment[...], cols)
        v.meta[0] = meta
        v.payload[ROWS:, :] = jnp.zeros((8, D), F32)
        v.payload[ROWS:, :ROWS] = meta
        for k in range(8):
            v.vecs[k : k + 1, :] = getattr(v, f"vector{k}")[...]
        for k in range(FF // D):
            v.vecs[8 + k : 9 + k, :] = v.up_bias[:, k * D : (k + 1) * D]
        v.tabs[...] = jnp.zeros((HEADS, 2 * SEQ), F32)
        for t in range(2):
            for head in range(HEADS):
                row, lane = t * 6 + head // 2, head % 2 * SEQ
                v.tabs[row : row + 1, lane : lane + NR] = v.rel[head, t : t + 1, :]

        @pl.when(section == 0)
        def _():
            for span in blocks():
                value = v.patches[span, :].astype(F32)
                v.x[span, :] = value
                v.payload[span, :] = value
            start("out_payload", "out_vecs", "out_tabs")
            forward([])
            wait(*in_wd)
            finish_layer()
            start("out_y", "out_output")
            wait("out_y", "out_output")

        @pl.when(section == 1)
        def _():
            for span in blocks():
                v.payload[span, :] = v.cotangent[span, :].astype(F32)
            start("out_payload", "out_vecs", "out_tabs")
            wait(*in_wq, "wo", *in_wu, *in_wd)

        wait("out_payload", "out_vecs", "out_tabs")

    def run_save():
        start("vecs", "tabs", *in_x, *in_meta, *in_wq, "wo", *in_wu)
        forward(in_x)
        wait(*stores)

    def run_own():
        start("vecs", "tabs", "b0", "meta0", *in_wq, "wo", *in_wu, "u_a0", *in_wd)
        forward(["b0"])
        wait("u_a0")
        backward_hidden()
        backward_middle()
        backward_attention()
        own_input_grad()
        store("out_grad")
        wait(*stores)

    def run_chunk():
        u_a, u_b = ([f"u_{side}{k}" for k in range(shards)] for side in "ab")
        in_b = [f"b{k}" for k in range(shards)]
        early = ["vecs", *u_b, "in_slope"]
        middle = [*in_wu, "in_normal2", "in_inverse2", "in_branch", "in_sel", "in_act_sel"]
        late = ["wo", "in_qkv", "in_probs"]
        own = ["a0", "meta0", "in_y", "in_output", *in_wq] if extras else []

        if saved:

            @pl.when(section == 0)
            def _():
                start(*early, *in_wd, *middle, *in_sums, *late, *own)
                wait(*early, *in_wd)

            @pl.when(section == 1)
            def _():
                start("vecs", "tabs", *in_b, *in_meta, *in_wq, "wo", *in_wu)
                start(*u_a, *in_wd, *in_sums)
                forward(in_b)
                wait(*u_a, *in_wd)
                if extras:
                    finish_layer()

        else:

            @pl.when(section == 0)
            def _():
                start(*in_x, *u_b)

            @pl.when(section == 1)
            def _():
                start(*in_b, *u_a)

            start("vecs", "tabs", *in_meta, *in_wq, "wo", *in_wu, *in_wd, *in_sums)
            forward(in_b)
            wait(*u_a)

        total_out = backward_hidden()

        if saved:
            pl.when(section == 0)(lambda: wait(*middle))

        wait(*in_sums)

        def add(name, where, value):
            ref = getattr(v, name)
            ref[where] = value if first else ref[where] + value

        everything = (slice(None), slice(None))
        add("sum_u", everything, dot(v.sel[2], v.dhid[...]))
        add("sum_d", everything, dot_lt(v.act_sel[...], v.dob[...]))
        if last:
            pack_rows(0)
        else:
            store("out_sum_u", "out_sum_d")
        totals = [total_out] + backward_middle()
        for k, total in enumerate(totals):
            add("sum_v", (slice(k, k + 1), slice(None)), column_sum(total))
        add("sum_o", everything, dot(v.sel[1], v.dbr[...]))
        if last:
            pack_rows(1)
        else:
            store("out_sum_o", "out_sum_v")

        if saved:
            pl.when(section == 0)(lambda: wait(*late))

        backward_attention()
        add("sum_q", everything, dot(v.sel[0], v.dqkv[...]))
        if last:
            pack_rows(2)
        else:
            store("out_sum_q")
        if extras:

            pl.when(section == 0)(lambda: wait(*own))
            store("out_y")
            own_extras()
            store("out_grad", "out_small")
        wait(*stores)

    def pack_rows(stage):
        core = lax.axis_index("dp") % 2
        half, quarter = SEL // 2, SELF // 8
        for side, target in enumerate(packs):
            whose = core if side == 0 else 1 - core
            low = pl.ds(pl.multiple_of(whose * half, 8), half)
            pieces = {}
            if stage == 0:
                pieces["u"] = (v.sum_u.at[low, :], target.at[:half, : 4 * D])
                for k in range(4):
                    start_row = pl.multiple_of(whose * (SELF // 2) + k * quarter, 8)
                    span = slice((8 + k) * D, (9 + k) * D)
                    piece = v.sum_d.at[pl.ds(start_row, quarter), :]
                    pieces[f"d{k}"] = (piece, target.at[:half, span])
            elif stage == 1:
                pieces["o"] = (v.sum_o.at[low, :], target.at[:half, 7 * D : 8 * D])
                tails = [v.sum_v.at[...], v.sum_o.at[SEL : SEL + 8, :]]
                tails += [v.sum_u.at[SEL : SEL + 8, k * D : (k + 1) * D] for k in range(FF // D)]
                for k, piece in enumerate(tails):
                    pieces[f"t{k}"] = (piece, target.at[half:, k * D : (k + 1) * D])
            else:
                pieces["q"] = (v.sum_q.at[low, :], target.at[:half, 4 * D : 7 * D])
            for name, piece in pieces.items():
                table[f"pack{side}{name}"] = piece
                store(f"pack{side}{name}")

    if kind == "fwd":
        run_first()
    elif kind == "save":
        pl.when(section == 0)(run_save)
    elif kind == "own":
        pl.when(section == 1)(run_own)
    else:
        run_chunk()


def run_layer(
    kind, vecs, tabs, weights, a_shards, b_shards=(), saved=(), output=None, sums=None, last=False
):
    shards = len(a_shards) if kind != "fwd" else 1
    hbm = pl.BlockSpec(memory_space=pl.ANY)
    smem = pl.BlockSpec(memory_space=pltpu.SMEM)
    extras, first = output is not None, sums is None
    ins = [vecs, tabs, *weights, *a_shards, *b_shards, *saved]
    if kind == "fwd":
        ins = [*a_shards, *weights]
    aliases = {}
    row_shape = jax.ShapeDtypeStruct((ROWS, D), F32)
    if kind == "fwd":
        outs = [
            jax.ShapeDtypeStruct((ROWS + 8, D), F32),
            jax.ShapeDtypeStruct((8 + FF // D, D), F32),
            jax.ShapeDtypeStruct((HEADS, 2 * SEQ), F32),
            row_shape,
            row_shape,
        ]
    elif kind == "own":
        outs = [row_shape]
    elif kind == "save":
        outs = saved_shapes(shards)
    else:
        if last:
            outs = [jax.ShapeDtypeStruct(PACK, F32)] * 2
        else:
            outs = [jax.ShapeDtypeStruct(shape, F32) for shape in SUM_SHAPES]
        if extras:
            ins += output
            outs += [jax.ShapeDtypeStruct((1, ROWS, D), F32)] * 2
            outs.append(jax.ShapeDtypeStruct((24, D), F32))
        if not first:
            if not last:
                aliases = {len(ins) + k: k for k in range(5)}
            ins += list(sums)
    return pl.pallas_call(
        functools.partial(layer_kernel, kind, shards, bool(saved), extras, first, last),
        out_shape=tuple(outs),
        in_specs=[smem if kind == "fwd" else hbm] + [hbm] * (len(ins) - 1),
        out_specs=(hbm,) * len(outs),
        scratch_shapes=[*Scratch(kind, shards).shapes, pltpu.SemaphoreType.DMA((96,))],
        input_output_aliases=aliases,
        compiler_params=pltpu.CompilerParams(vmem_limit_bytes=60 * 1024 * 1024),
        cost_estimate=pl.CostEstimate(
            flops=WORK[kind] * shards * ROWS, bytes_accessed=1000, transcendentals=0
        ),
        name="layer_" + kind,
    )(*ins)


def finish_kernel(kept, received, small_a, small_b, small_c, small_d, *outs):
    outs, (mine, other, sems) = outs[:-3], outs[-3:]
    grad_q, grad_o, grad_u, grad_d, grad_ub, grad_table, *vectors = outs
    half = SEL // 2
    spans = [slice(0, 4 * D), slice(4 * D, 8 * D), slice(8 * D, 12 * D)]
    copies = []
    for k, span in enumerate(spans):
        copies.append(
            [
                pltpu.make_async_copy(kept.at[:, span], mine.at[:, span], sems.at[2 * k]),
                pltpu.make_async_copy(received.at[:, span], other.at[:, span], sems.at[2 * k + 1]),
            ]
        )
        for one in copies[-1]:
            one.start()
    device = lax.axis_index("dp")

    def total(lines, lanes):
        return mine[lines, lanes] + other[lines, lanes]

    body_rows, tail_rows = slice(0, half), slice(half, half + 8)
    for one in copies[0]:
        one.wait()
    grad_u[0] = total(body_rows, spans[0])
    for one in copies[1]:
        one.wait()
    sums_low, sums_out = (total(tail_rows, slice(k * D, (k + 1) * D)) for k in range(2))
    sums_up = [total(tail_rows, slice((2 + k) * D, (3 + k) * D))[:1] for k in range(FF // D)]
    small_all = (small_a[...] + small_b[...]) + (small_c[...] + small_d[...])
    small = [small_all[:8], small_all[8:16]]
    width = vectors[0].shape[1]
    sources = (
        (small[0], 1),
        (small[0], 2),
        (sums_out, 0),
        (sums_low, 3),
        (sums_low, 1),
        (sums_low, 2),
        (sums_low, 0),
        (small[0], 0),
    )
    for out, (source, line) in zip(vectors, sources):
        out[...] = pltpu.roll(source, D - device * width, 1)[line : line + 1, :width]
    wide = grad_ub.shape[1]
    first = device * wide
    row = sums_up[0]
    for k in range(1, FF // D):
        row = jnp.where(first // D == k, sums_up[k], row)
    turned = pltpu.roll(jnp.broadcast_to(row, (8, D)), D - first % D, 1)
    grad_ub[...] = turned[:1, :wide]
    grad_q[0] = total(body_rows, slice(4 * D, 7 * D))
    grad_o[0] = total(body_rows, slice(7 * D, 8 * D))
    for one in copies[2]:
        one.wait()
    heads_low, heads_high = small[1], small_all[16:]
    for t in range(2):
        span = slice(32 * t, 32 * t + NR)
        for head in range(HEADS):
            held = heads_low if head < 8 else heads_high
            grad_table[0, head, t : t + 1, :] = held[head % 8 : head % 8 + 1, span]
    for k in range(4):
        grad_d[0, k * half : (k + 1) * half, :] = total(
            body_rows, slice((8 + k) * D, (9 + k) * D)
        )


def body(
    patches,
    cotangent,
    seg_ids,
    grid_cols,
    norm_gain1,
    norm_bias1,
    qkv_weight,
    out_weight,
    out_bias,
    attn_scale,
    norm_gain2,
    norm_bias2,
    up_weight,
    up_bias,
    down_weight,
    down_bias,
    mlp_scale,
    rel_table,
):
    dp_count = lax.axis_size("dp")
    supers = dp_count // (2 * BLOCK)
    section = lax.axis_index("section")
    device = lax.axis_index("dp")
    core = device % 2
    def pairs(move):
        return [
            (2 * (b * supers + s) + c, 2 * (move(b) * supers + s) + c)
            for b in range(BLOCK)
            for s in range(supers)
            for c in range(2)
        ]

    def along(array, step):
        return lax.ppermute(array, "dp", pairs(lambda b: (b // 2 + step) % 4 * 2 + b % 2))

    def across(array):
        return lax.ppermute(array, "dp", pairs(lambda b: b ^ 1))

    def diagonal(array):
        moves = [(source, target ^ 1) for source, target in pairs(lambda b: b ^ 1)]
        return lax.ppermute(array, "dp", moves)

    def sibling(array):
        return lax.ppermute(array, "dp", [(d, d ^ 1) for d in range(dp_count)])

    vectors = (
        norm_gain1,
        norm_bias1,
        out_bias,
        attn_scale,
        norm_gain2,
        norm_bias2,
        down_bias,
        mlp_scale,
        up_bias,
    )
    weights = (qkv_weight[0], out_weight[0], up_weight[0], down_weight[0])

    def after(array, *others):
        return lax.optimization_barrier((array, *others))[0]

    firsts = [
        grid_cols,
        seg_ids.reshape(1, ROWS),
        rel_table[0].transpose(1, 0, 2),
        patches,
        cotangent,
        *vectors,
    ]
    own, vecs, tabs, y0, output0 = run_layer("fwd", None, None, weights, firsts)

    def layer(kind, *rest, **named):
        return run_layer(kind, vecs, tabs, weights, *rest, **named)

    def flipped(array, flip):
        return lax.ppermute(array, "dp", pairs(lambda b: b ^ flip))

    x1 = lax.ppermute(y0, "section", [(0, 1)])
    a_y = across(own)
    a_z = [along(own, step) for step in (1, 3, 2)]
    (grad1,) = layer("own", [own], [x1])
    u0 = lax.ppermute(grad1, "section", [(1, 0)])
    own_then = after(own, grad1)
    kept = layer("save", [own_then, a_y])
    a_yz = [across(after(piece, kept[0])) for piece in a_z[:2]]
    b_own = jnp.where(section == 0, after(u0, kept[0], a_z[2]), x1)
    b_y = across(b_own)
    b_z = [along(b_own, step) for step in (1, 3)]
    b_z.append(along(after(b_own, b_y, *a_yz), 2))
    a_yz.append(across(after(a_z[2], b_y, *a_yz)))
    *sums, section_out, section_grad, small = layer(
        "chunk",
        [own, a_y],
        [b_own, b_y],
        (after(kept[0], *a_yz[:2]), *kept[1:]),
        (y0, output0),
    )
    b_z = [after(piece, small) for piece in b_z]
    b_yz = [across(piece) for piece in b_z]
    moved = flipped(small, 4)
    sums = layer("chunk", [after(a_z[0], a_yz[2]), *a_z[1:]], b_z, (), None, sums)
    small = small + after(moved, sums[0])
    moved = flipped(small, 2)
    last_a = [after(a_yz[0], small), *a_yz[1:]]
    sums = layer("chunk", last_a, b_yz, (), None, sums, supers == 1)
    small = small + after(moved, sums[0])
    width = D // dp_count
    wide = FF // dp_count
    if supers == 1:
        mine, others = sums
        hbm = pl.BlockSpec(memory_space=pl.ANY)
        shapes = [(1, width, 3 * D), (1, width, D), (1, width, FF), (1, wide, D), (1, wide)]
        shapes += [(1, HEADS, 2, NR)] + [(1, width)] * 8
        grad_q, grad_o, grad_u, grad_d, grad_ub, grad_table, *vectors = pl.pallas_call(
            finish_kernel,
            out_shape=tuple(jax.ShapeDtypeStruct(shape, F32) for shape in shapes),
            in_specs=[hbm, hbm] + [pl.BlockSpec()] * 4,
            scratch_shapes=[
                pltpu.VMEM(PACK, F32),
                pltpu.VMEM(PACK, F32),
                pltpu.SemaphoreType.DMA((6,)),
            ],
            compiler_params=pltpu.CompilerParams(vmem_limit_bytes=32 * 1024 * 1024),
            name="finish",
        )(mine, sibling(others), small, across(small), sibling(small), diagonal(small))
        grad_table = grad_table.transpose(0, 2, 1, 3)
    else:
        sum_u, sum_d, sum_o, sum_q, sum_v = sums
        sum_v = jnp.concatenate(
            [sum_v[:4], sum_o[SEL : SEL + 1], sum_u[SEL : SEL + 1].reshape(FF // D, D)], axis=0
        )

        def shifted(array, step):
            moves = [
                (2 * (b * supers + s) + c, 2 * (b * supers + (s + step) % supers) + c)
                for b in range(BLOCK)
                for s in range(supers)
                for c in range(2)
            ]
            return lax.ppermute(array, "dp", moves)

        def scatter(partial):
            parts = partial.reshape(supers, 2, partial.shape[0] // (2 * supers), partial.shape[1])
            held = lax.dynamic_index_in_dim(parts, core, 1, keepdims=False)
            held = held + sibling(lax.dynamic_index_in_dim(parts, 1 - core, 1, keepdims=False))
            place = device // 2 % supers
            total = lax.dynamic_index_in_dim(held, place, 0, keepdims=False)
            for step in range(1, supers):
                there = (place + step) % supers
                total = total + shifted(
                    lax.dynamic_index_in_dim(held, there, 0, keepdims=False), step
                )
            return total[None]

        small = small + across(small)
        sums = jnp.concatenate([sum_v, small[:8], small[8:]], axis=0)
        sums = sums + sibling(sums)
        sums = sums + sum(shifted(sums, step) for step in range(1, supers))
        vectors = [
            lax.dynamic_slice(sums, (row, device * width), (1, width))
            for row in (10, 11, 4, 3, 1, 2, 0, 9)
        ]
        grad_ub = lax.dynamic_slice(sums[5:9].reshape(1, FF), (0, device * wide), (1, wide))
        grad_table = sums[17 : 17 + HEADS, :64].reshape(HEADS, 2, 32)[:, :, :NR]
        grad_table = grad_table.transpose(1, 0, 2)[None]
        grad_q, grad_o, grad_u, grad_d = (
            scatter(partial) for partial in (sum_q[:SEL], sum_o[:SEL], sum_u[:SEL], sum_d)
        )
    gain1, bias1, out_b, attn, gain2, bias2, down_b, mlp = vectors
    return (
        section_out,
        section_grad,
        gain1,
        bias1,
        grad_q,
        grad_o,
        out_b,
        attn,
        gain2,
        bias2,
        grad_u,
        grad_ub,
        grad_d,
        down_b,
        mlp,
        grad_table,
    )


def solution(mesh):
    row, whole = P("dp", None), P("section", None)
    matrix = P("section", None, None)
    in_specs = (
        row,
        row,
        P("dp"),
        row,
        whole,
        whole,
        matrix,
        matrix,
        whole,
        whole,
        whole,
        whole,
        matrix,
        whole,
        matrix,
        whole,
        whole,
        P("section", None, None, None),
    )
    tokens, vector, weight = P("section", "dp", None), P("section", "dp"), P("section", "dp", None)
    out_specs = (
        tokens,
        tokens,
        vector,
        vector,
        weight,
        weight,
        vector,
        vector,
        vector,
        vector,
        weight,
        vector,
        weight,
        vector,
        vector,
        P("section", None, None, None),
    )
    return jax.shard_map(body, mesh=mesh, in_specs=in_specs, out_specs=out_specs, check_vma=False)
```
